128 devices in a mesh: param: 8 (over y, core), ex: 16 (over z, x).
Axes of the slice: x: 4, y: 4, z: 4, core: 2. Of those that a mesh axis runs over, the one named last changes fastest.
Arguments:
- activations: bfloat16 [1024, 128, 8192], P('ex', None, 'param'), may hold values from -8 to 8
- cotangents: bfloat16 [1024, 128, 64], P('ex'), may hold values from -8 to 8
- token_ids: int32 [1024, 128], P('ex'), may hold values from 0 to 128255, as said below
- signs: int32 [64, 8192], P(None, 'param'), may hold values from -1 to 1, as said below
- select: int32 [32768], replicated, may hold values from 0 to 524287, as said below
Outputs:
- features: float32 [1024, 32768], P('ex', 'param')
- gram: float32 [1024, 1024], P('ex')
The draws below stay inside these ranges and needn't reach their ends.
Inputs may be any that keep to these rules, and one draw needn't show every extreme that they name: `token_ids`: in each example the nonzero ids come first and zeros fill the rest; at least 32 positions of every example are nonzero. `signs`: every entry is 1 or -1. `select`: the 32768 entries are distinct.
All inputs are finite; a program needn't handle non-finite values.
Results may differ from the reference program's by a relative error of at most 0.0003.
Values sent between devices are 32-bit elements; how exact they have to be, the bound alone decides.
No kernel may reach another device: no remote copies, remote signals or barrier semaphores. Data moves between devices by JAX's collectives and lax.ppermute only.
A program may use at most 192 MiB of HBM per device.

```python
import math
import jax
import jax.numpy as jnp
from jax import lax

D = 8192
VOCAB = 128256
SLAB = 64
TOKS = 128
K = 32768
EX = 1024


def mixed_field(key, shape_common, shape_whole):
    common = jax.random.normal(jax.random.fold_in(key, 11), shape_common, jnp.float32)
    private = jax.random.normal(jax.random.fold_in(key, 12), shape_whole, jnp.float32)
    values = (common[None] + private) * 0.7071
    return jnp.clip(values, -8.0, 8.0)


def draw_activations(key, part):
    return mixed_field(key, (TOKS, D), (EX, TOKS, D)).astype(jnp.bfloat16)


def draw_cotangents(key, part):
    return mixed_field(key, (TOKS, SLAB), (EX, TOKS, SLAB)).astype(jnp.bfloat16)


def draw_token_ids(key, part):
    lengths = jax.random.randint(jax.random.fold_in(key, 21), (EX,), TOKS // 4, TOKS + 1)
    token_values = jax.random.randint(jax.random.fold_in(key, 22), (EX, TOKS), 1, VOCAB)
    positions = jnp.arange(TOKS, dtype=jnp.int32)[None, :]
    return jnp.where(positions < lengths[:, None], token_values, 0).astype(jnp.int32)


def draw_signs(key, part):
    coins = jax.random.randint(jax.random.fold_in(key, 31), (SLAB, D), 0, 2)
    return (2 * coins - 1).astype(jnp.int32)


def draw_select(key, part):
    shuffled = jax.random.permutation(jax.random.fold_in(key, 41), SLAB * D - 2) + 1
    chosen = jnp.concatenate([shuffled[:K - 2].astype(jnp.int32), jnp.array([0, SLAB * D - 1], jnp.int32)])
    order = jax.random.permutation(jax.random.fold_in(key, 42), K)
    return chosen[order].astype(jnp.int32)


def setup_inputs(seed: int = 0) -> dict:
    streams_of = jax.random.split(jax.random.key(seed), 6)
    activations = draw_activations(jax.random.fold_in(streams_of[5], 71), 0)
    cotangents = draw_cotangents(jax.random.fold_in(streams_of[5], 71), 0)
    token_ids = draw_token_ids(jax.random.fold_in(streams_of[5], 71), 0)
    signs = draw_signs(jax.random.fold_in(streams_of[5], 71), 0)
    select = draw_select(jax.random.fold_in(streams_of[5], 71), 0)
    return {"activations": activations, "cotangents": cotangents, "token_ids": token_ids, "signs": signs, "select": select}


def walsh_rows(values):
    lead_rows = values.shape[0]
    length = values.shape[1]
    half_width = 1
    while half_width < length:
        paired = values.reshape(lead_rows, length // (2 * half_width), 2, half_width)
        first = paired[:, :, 0, :]
        second = paired[:, :, 1, :]
        values = jnp.stack([first + second, first - second], axis=2).reshape(lead_rows, length)
        half_width = half_width * 2
    return values

def reference(activations, cotangents, token_ids, signs, select):
    group = math.gcd(EX, 8)
    live_mask = token_ids != 0
    masked = jnp.where(live_mask[:, :, None], cotangents, jnp.zeros((), cotangents.dtype))
    flip_sign = signs.astype(jnp.float32).reshape(-1)

    def one_group(pair):
        acts, cots = pair
        gradient = jnp.einsum('etr,etc->erc', cots.astype(jnp.float32), acts.astype(jnp.float32), precision=lax.Precision.HIGHEST) * (1.0 / math.sqrt(TOKS))
        flipped = gradient.reshape(group, SLAB * D) * flip_sign[None, :]
        transformed = walsh_rows(flipped)
        return jnp.take(transformed, select, axis=1) / math.sqrt(SLAB * D)
    grouped = lax.map(one_group, (activations.reshape(EX // group, group, TOKS, D), masked.reshape(EX // group, group, TOKS, SLAB)))
    features = grouped.reshape(EX, K)
    gram = jnp.dot(features, features.T, precision=lax.Precision.HIGHEST, preferred_element_type=jnp.float32) / K
    return (features, gram)
```

```python
import functools
import math

import jax
import jax.numpy as jnp
from jax import lax
from jax.experimental import pallas as pl
from jax.experimental.pallas import tpu as pltpu
from jax.sharding import PartitionSpec as P

D = 8192
SLAB = 64
TOKS = 128
K = 32768
LANES = 128
STEP_EX = 8
TAP = 256


def walsh_table(table_order):
    row_index = lax.broadcasted_iota(jnp.int32, (table_order, table_order), 0)
    column_index = lax.broadcasted_iota(jnp.int32, (table_order, table_order), 1)
    common_bits = row_index & column_index
    parity = jnp.zeros((table_order, table_order), jnp.int32)
    for bit_index in range(table_order.bit_length() - 1):
        parity = parity ^ common_bits >> bit_index & 1
    return (1 - 2 * parity).astype(jnp.float32)


def butterfly(parts):
    count = len(parts)
    half = 1
    while half < count:
        out = list(parts)
        for index in range(count):
            if not index & half:
                out[index] = parts[index] + parts[index | half]
                out[index | half] = parts[index] - parts[index | half]
        parts = out
        half *= 2
    return parts


def local_kernel(n_ex, width, n_feat, rows_ref, acts_ref, cots_ref, flip_ref, walsh_ref, half_ref, sign_ref,
                 out_ref, grad_ref, table_ref, buf_ref):
    step = pl.program_id(0)
    tiles = width // LANES
    rows = SLAB

    @pl.loop(0, STEP_EX)
    def _(i):
        e = step * STEP_EX + i
        g = jnp.dot(cots_ref[i], acts_ref[i], preferred_element_type=jnp.float32)
        g = g * flip_ref[...]
        for low in range(2):
            tile = [g[:, (2 * q + low) * LANES:(2 * q + low + 1) * LANES] for q in range(tiles // 2)]
            tile = butterfly(tile)
            for q in range(tiles // 2):
                parts = butterfly([tile[q][8 * s:8 * s + 8] for s in range(rows // 8)])
                for s in range(rows // 8):
                    grad_ref[2 * q + low, pl.ds(e * rows + 8 * s, 8), :] = parts[s]

    @pl.when(step == pl.num_programs(0) - 1)
    def _():
        lane = lax.broadcasted_iota(jnp.int32, (TAP, LANES), 1)
        low_half = jnp.where(lane < LANES // 2, 1.0, -1.0).astype(jnp.float32)

        @pl.loop(0, (rows // 8) * (tiles // 2))
        def _(index):
            s = index // (tiles // 2)
            q = index % (tiles // 2)
            high, low = [], []
            for r in range(8):
                pieces = [
                    grad_ref.at[2 * q + j][pl.ds(s * 8 + r, n_ex, stride=rows), :] for j in range(2)
                ]
                x = jnp.concatenate(pieces, axis=1)
                h = x.astype(jnp.bfloat16)
                high.append(h)
                low.append((x - h.astype(jnp.float32)).astype(jnp.bfloat16))
            nt = (((1,), (1,)), ((), ()))
            mixed = lax.dot_general(walsh_ref[...], jnp.concatenate(high, axis=0), nt, preferred_element_type=jnp.float32)
            mixed += lax.dot_general(walsh_ref[...], jnp.concatenate(low, axis=0), nt, preferred_element_type=jnp.float32)
            parts = butterfly([mixed[:, j * LANES:(j + 1) * LANES] for j in range(4)])
            for j in range(4):
                v = parts[j]
                v = v * low_half + pltpu.roll(v, LANES // 2, 1)
                table_ref[pl.ds((s * 4 + j) * width + q * TAP, TAP), :] = v

        @pl.loop(0, n_feat // LANES)
        def _(block):
            base = pl.multiple_of(block * LANES, LANES)
            for j in range(LANES):
                buf_ref[j:j + 1, :] = table_ref[pl.ds(rows_ref[base + j], 1), :]
            t = buf_ref[...].T
            here = pl.ds(base, LANES)
            picked = jnp.where(half_ref[:, here] > 0, t[LANES // 2:], t[:LANES // 2])
            out_ref[:, here] = picked * sign_ref[:, here]


def local_terms(activations, cots, flip, rows, half, sign):
    n_ex, toks, width = activations.shape
    slab = cots.shape[1]
    n_feat = rows.shape[0]
    walsh = walsh_table(TAP).astype(jnp.bfloat16)
    whole = lambda shape: pl.BlockSpec(shape, lambda i, *_: (0,) * len(shape))
    return pl.pallas_call(
        functools.partial(local_kernel, n_ex, width, n_feat),
        out_shape=jax.ShapeDtypeStruct((n_ex, n_feat), jnp.float32),
        grid_spec=pltpu.PrefetchScalarGridSpec(
            num_scalar_prefetch=1,
            grid=(n_ex // STEP_EX,),
            in_specs=[
                pl.BlockSpec((STEP_EX, toks, width), lambda i, *_: (i, 0, 0)),
                pl.BlockSpec((STEP_EX, slab, toks), lambda i, *_: (i, 0, 0)),
                whole((slab, width)),
                whole((TAP, TAP)),
                whole((1, n_feat)),
                whole((1, n_feat)),
            ],
            out_specs=whole((n_ex, n_feat)),
            scratch_shapes=[
                pltpu.VMEM((width // LANES, n_ex * slab, LANES), jnp.float32),
                pltpu.VMEM((slab // 2 * width, LANES), jnp.float32),
                pltpu.VMEM((LANES, LANES), jnp.float32),
            ],
        ),
        compiler_params=pltpu.CompilerParams(
            dimension_semantics=("arbitrary",), vmem_limit_bytes=60 * 1024 * 1024
        ),
        name="local_terms",
    )(rows, activations, cots, flip, walsh, half, sign)


def prepare(cotangents, token_ids, signs, select, my_index, width, section_bits):
    live = token_ids != 0
    cots = jnp.where(live[:, None, :], jnp.swapaxes(cotangents, 1, 2), jnp.zeros((), cotangents.dtype))
    factor = 1.0 / math.sqrt(TOKS) / math.sqrt(SLAB * D)
    flip = signs.astype(jnp.float32) * factor
    column = select % D
    row = select // D
    rows = (row >> 1) * width + column % width
    shared = (column // width) & my_index
    parity = jnp.zeros_like(shared)
    for bit_index in range(section_bits):
        parity = parity ^ shared >> bit_index & 1
    sign = (1 - 2 * parity).astype(jnp.float32)
    return cots, flip, rows, (row & 1)[None, :], sign[None, :]


def body(activations, cotangents, token_ids, signs, select):
    highest = lax.Precision.HIGHEST
    section_bits = lax.axis_size("param").bit_length() - 1
    cots, flip, rows, half, sign = prepare(
        cotangents, token_ids, signs, select, lax.axis_index("param"), activations.shape[2], section_bits
    )
    partial_term = local_terms(activations, cots, flip, rows, half, sign)
    features = lax.psum_scatter(partial_term, "param", scatter_dimension=1, tiled=True)
    tile_block = jnp.einsum(
        "ek,fk->ef", features, lax.all_gather(features, "ex", axis=0, tiled=True), precision=highest
    )
    gram = lax.psum(tile_block, "param") / K
    return (features, gram)


def solution(mesh):
    return jax.shard_map(
        body,
        mesh=mesh,
        in_specs=(
            P("ex", None, "param"),
            P("ex", None, None),
            P("ex", None),
            P(None, "param"),
            P(),
        ),
        out_specs=(P("ex", "param"), P("ex", None)),
        check_vma=False,
    )
```

```python
import functools
import math

import jax
import jax.numpy as jnp
from jax import lax
from jax.experimental import pallas as pl
from jax.experimental.pallas import tpu as pltpu
from jax.sharding import PartitionSpec as P

D = 8192
SLAB = 64
TOKS = 128
K = 32768
LANES = 128
STEP_EX = 8
TAP = 256
CHUNKS = 2


def walsh_table(table_order):
    row_index = lax.broadcasted_iota(jnp.int32, (table_order, table_order), 0)
    column_index = lax.broadcasted_iota(jnp.int32, (table_order, table_order), 1)
    common_bits = row_index & column_index
    parity = jnp.zeros((table_order, table_order), jnp.int32)
    for bit_index in range(table_order.bit_length() - 1):
        parity = parity ^ common_bits >> bit_index & 1
    return (1 - 2 * parity).astype(jnp.float32)


def butterfly(parts):
    count = len(parts)
    half = 1
    while half < count:
        out = list(parts)
        for index in range(count):
            if not index & half:
                out[index] = parts[index] + parts[index | half]
                out[index | half] = parts[index] - parts[index | half]
        parts = out
        half *= 2
    return parts


def table_kernel(n_ex, width, acts_ref, cots_ref, flip_ref, walsh_ref, table_ref, grad_ref):
    step = pl.program_id(0)
    tiles = width // LANES
    rows = SLAB

    @pl.loop(0, STEP_EX)
    def _(i):
        e = step * STEP_EX + i
        g = jnp.dot(cots_ref[i], acts_ref[i], preferred_element_type=jnp.float32)
        g = g * flip_ref[...]
        for low in range(2):
            tile = [g[:, (2 * q + low) * LANES:(2 * q + low + 1) * LANES] for q in range(tiles // 2)]
            tile = butterfly(tile)
            for q in range(tiles // 2):
                parts = butterfly([tile[q][8 * s:8 * s + 8] for s in range(rows // 8)])
                for s in range(rows // 8):
                    grad_ref[2 * q + low, pl.ds(e * rows + 8 * s, 8), :] = parts[s]

    @pl.when(step == pl.num_programs(0) - 1)
    def _():
        lane = lax.broadcasted_iota(jnp.int32, (TAP, LANES), 1)
        low_half = jnp.where(lane < LANES // 2, 1.0, -1.0).astype(jnp.float32)

        @pl.loop(0, (rows // 8) * (tiles // 2))
        def _(index):
            s = index // (tiles // 2)
            q = index % (tiles // 2)
            high, low = [], []
            for r in range(8):
                pieces = [
                    grad_ref.at[2 * q + j][pl.ds(s * 8 + r, n_ex, stride=rows), :] for j in range(2)
                ]
                x = jnp.concatenate(pieces, axis=1)
                h = x.astype(jnp.bfloat16)
                high.append(h)
                low.append((x - h.astype(jnp.float32)).astype(jnp.bfloat16))
            nt = (((1,), (1,)), ((), ()))
            mixed = lax.dot_general(walsh_ref[...], jnp.concatenate(high, axis=0), nt, preferred_element_type=jnp.float32)
            mixed += lax.dot_general(walsh_ref[...], jnp.concatenate(low, axis=0), nt, preferred_element_type=jnp.float32)
            parts = butterfly([mixed[:, j * LANES:(j + 1) * LANES] for j in range(4)])
            for j in range(4):
                v = parts[j]
                v = v * low_half + pltpu.roll(v, LANES // 2, 1)
                table_ref[pl.ds((s * 4 + j) * width + q * TAP, TAP), :] = v


def gather_kernel(n_block, rows_ref, table_ref, half_ref, sign_ref, out_ref, buf_ref):
    @pl.loop(0, n_block)
    def _(block):
        base = pl.multiple_of(block * LANES, LANES)
        for j in range(LANES):
            buf_ref[j:j + 1, :] = table_ref[pl.ds(rows_ref[base + j], 1), :]
        t = buf_ref[...].T
        here = pl.ds(block, 1)
        picked = jnp.where(half_ref[here, :] > 0, t[LANES // 2:], t[:LANES // 2])
        out_ref[block] = picked * sign_ref[here, :]


def whole(shape):
    return pl.BlockSpec(shape, lambda i, *_: (0,) * len(shape))


def make_table(activations, cots, flip):
    n_ex, toks, width = activations.shape
    slab = cots.shape[1]
    walsh = walsh_table(TAP).astype(jnp.bfloat16)
    return pl.pallas_call(
        functools.partial(table_kernel, n_ex, width),
        out_shape=pltpu.VMEM((slab // 2 * width, LANES), jnp.float32),
        grid=(n_ex // STEP_EX,),
        in_specs=[
            pl.BlockSpec((STEP_EX, toks, width), lambda i: (i, 0, 0)),
            pl.BlockSpec((STEP_EX, slab, toks), lambda i: (i, 0, 0)),
            whole((slab, width)),
            whole((TAP, TAP)),
        ],
        out_specs=pl.BlockSpec(memory_space=pltpu.VMEM),
        scratch_shapes=[pltpu.VMEM((width // LANES, n_ex * slab, LANES), jnp.float32)],
        compiler_params=pltpu.CompilerParams(
            dimension_semantics=("arbitrary",), vmem_limit_bytes=30 * 1024 * 1024
        ),
        name="make_table",
    )(activations, cots, flip, walsh)


def gather_rows(table, rows, half, sign):
    n_block = half.shape[0]
    return pl.pallas_call(
        functools.partial(gather_kernel, n_block),
        out_shape=jax.ShapeDtypeStruct((n_block, LANES // 2, LANES), jnp.float32),
        in_specs=[
            pl.BlockSpec(memory_space=pltpu.SMEM),
            pl.BlockSpec(memory_space=pltpu.VMEM),
            pl.BlockSpec(memory_space=pltpu.VMEM),
            pl.BlockSpec(memory_space=pltpu.VMEM),
        ],
        out_specs=pl.BlockSpec(memory_space=pltpu.VMEM),
        scratch_shapes=[pltpu.VMEM((LANES, LANES), jnp.float32)],
        compiler_params=pltpu.CompilerParams(vmem_limit_bytes=16 * 1024 * 1024),
        name="gather_rows",
    )(rows.reshape(-1), table, half, sign)


def prepare(cotangents, token_ids, signs, select, my_index, width, section_bits):
    live = token_ids != 0
    cots = jnp.where(live[:, None, :], jnp.swapaxes(cotangents, 1, 2), jnp.zeros((), cotangents.dtype))
    factor = 1.0 / math.sqrt(TOKS) / math.sqrt(SLAB * D)
    flip = signs.astype(jnp.float32) * factor
    column = select % D
    row = select // D
    rows = (row >> 1) * width + column % width
    shared = (column // width) & my_index
    parity = jnp.zeros_like(shared)
    for bit_index in range(section_bits):
        parity = parity ^ shared >> bit_index & 1
    sign = (1 - 2 * parity).astype(jnp.float32)
    return cots, flip, rows, row & 1, sign


def test_local(a, c, t, s, sel, my):
    cots, flip, rows, half, sign = prepare(c, t, s, sel, my, a.shape[2], 3)
    table = make_table(a, cots, flip)
    out = gather_rows(table, rows, half.reshape(-1, LANES), sign.reshape(-1, LANES))
    return jnp.swapaxes(out, 0, 1).reshape(64, -1)


def gram_kernel(n_ex, *refs):
    x_refs, out_ref, high_ref, low_ref = refs[:-3], refs[-3], refs[-2], refs[-1]
    blocks = x_refs[0].shape[0]
    width = sum(r.shape[2] for r in x_refs)
    for b in range(blocks):
        x = jnp.concatenate([r[b] for r in x_refs], axis=1)
        h = x.astype(jnp.bfloat16)
        low = (x - h.astype(jnp.float32)).astype(jnp.bfloat16)
        for at in ((b, b + blocks) if b < 10 else (b,)):
            high_ref[at * n_ex:(at + 1) * n_ex, :] = h
            low_ref[at * n_ex:(at + 1) * n_ex, :] = low
    half = LANES // 2
    left = lax.broadcasted_iota(jnp.int32, (n_ex // 2, LANES), 1) < half
    nt = (((1,), (1,)), ((), ()))

    @pl.loop(0, blocks)
    def _(b):
        first = pl.multiple_of(b * n_ex, n_ex)
        mine = pl.ds(first, n_ex)
        near = pl.ds(first, 10 * n_ex)
        t = lax.dot_general(high_ref[mine, :], high_ref[near, :], nt, preferred_element_type=jnp.float32)
        t += lax.dot_general(high_ref[mine, :], low_ref[near, :], nt, preferred_element_type=jnp.float32)
        t += lax.dot_general(low_ref[mine, :], high_ref[near, :], nt, preferred_element_type=jnp.float32)
        for p in range(8):
            q = (p + 1) // 2
            top = t[:n_ex // 2, q * LANES:(q + 1) * LANES]
            low = t[n_ex // 2:, q * LANES:(q + 1) * LANES]
            if p % 2:
                low = pltpu.roll(low, half, 1)
            else:
                top = pltpu.roll(top, half, 1)
            out_ref[p, b, :n_ex // 2, :] = jnp.where(left, top, low)
            out_ref[p, b, n_ex // 2:, :] = t[8 * p:8 * p + 8, :LANES]


def partial_gram(parts):
    blocks, n_ex, _ = parts[0].shape
    width = sum(x.shape[2] for x in parts)
    vmem = pl.BlockSpec(memory_space=pltpu.VMEM)
    return pl.pallas_call(
        functools.partial(gram_kernel, n_ex),
        out_shape=jax.ShapeDtypeStruct((8, blocks, n_ex // 2 + 8, LANES), jnp.float32),
        in_specs=[vmem] * len(parts),
        out_specs=vmem,
        scratch_shapes=[pltpu.VMEM(((blocks + 10) * n_ex, width), jnp.bfloat16)] * 2,
        compiler_params=pltpu.CompilerParams(vmem_limit_bytes=16 * 1024 * 1024),
        name="partial_gram",
    )(*parts)


def sum_kernel(scale, x_ref, tile_ref, strip_ref):
    half = LANES // 2
    total = jnp.sum(x_ref[...], axis=0) * scale
    pair = total[:half // 2]
    tile = jnp.concatenate([pair[:, :half], pair[:, half:]], axis=0)
    tile_ref[0] = tile
    tile_ref[1] = tile.T
    strip_ref[...] = total[half // 2:]


def sum_tiles(received):
    vmem = pl.BlockSpec(memory_space=pltpu.VMEM)
    return pl.pallas_call(
        functools.partial(sum_kernel, 1.0 / K),
        out_shape=(
            jax.ShapeDtypeStruct((2, LANES // 2, LANES // 2), jnp.float32),
            jax.ShapeDtypeStruct((8, LANES), jnp.float32),
        ),
        in_specs=[vmem],
        out_specs=(vmem, vmem),
        compiler_params=pltpu.CompilerParams(vmem_limit_bytes=16 * 1024 * 1024),
        name="sum_tiles",
    )(received)


def place_kernel(me_ref, x_ref, out_ref):
    half = LANES // 2
    count = out_ref.shape[1] // half
    columns = [None] * count
    columns[0] = jnp.concatenate([x_ref[p, half:, :half] for p in range(8)], axis=0)
    for p in range(8):
        columns[p + 1] = x_ref[p, :half, :half]
        if count - 1 - p > p + 1:
            columns[count - 1 - p] = x_ref[p, :half, half:]
    row = jnp.concatenate(columns, axis=1)
    out_ref[...] = pltpu.roll(row, me_ref[0] * half, 1)


def place_tiles(tiles, me, n_ex, count):
    vmem = pl.BlockSpec(memory_space=pltpu.VMEM)
    return pl.pallas_call(
        place_kernel,
        out_shape=jax.ShapeDtypeStruct((n_ex, count * n_ex), jnp.float32),
        in_specs=[pl.BlockSpec(memory_space=pltpu.SMEM), vmem],
        out_specs=vmem,
        name="place_tiles",
    )(me.reshape(1), tiles)


def body(activations, cotangents, token_ids, signs, select):
    n_param, n_group = lax.axis_size("param"), lax.axis_size("ex")
    n_ex, _, width = activations.shape
    me = lax.axis_index("param")
    section_bits = n_param.bit_length() - 1
    cots, flip, rows, half, sign = prepare(cotangents, token_ids, signs, select, me, width, section_bits)
    table = make_table(activations, cots, flip)

    n_y = n_param // 2
    other_first = me % 2 == 0

    def arrange(x):
        x = x.reshape(n_y, 2, CHUNKS, n_group, -1)
        even, odd = x[:, 0], x[:, 1]
        x = jnp.stack([jnp.where(other_first, odd, even), jnp.where(other_first, even, odd)])
        return jnp.moveaxis(x, 2, 0).reshape(CHUNKS, 2, n_y * n_group * x.shape[-1] // LANES, LANES)

    rows, half, sign = arrange(rows), arrange(half), arrange(sign)
    swap = [(i, i ^ 1) for i in range(n_param)]
    ring = [[2 * y + core for y in range(n_y)] for core in range(2)]
    features, shares = [], []
    for chunk in range(CHUNKS):
        sent = gather_rows(table, rows[chunk, 0], half[chunk, 0], sign[chunk, 0])
        arrived = lax.ppermute(sent, "param", swap)
        kept = gather_rows(table, rows[chunk, 1], half[chunk, 1], sign[chunk, 1])
        pair = (kept + arrived).reshape(n_y, -1, n_ex, LANES)
        parts = lax.all_to_all(pair, "param", split_axis=0, concat_axis=0, axis_index_groups=ring)
        block = parts[0] + parts[1] + parts[2] + parts[3]
        features.append(block)
        shares.append(lax.all_to_all(block, "ex", split_axis=0, concat_axis=0))
    whole_features = jnp.swapaxes(jnp.concatenate(features, axis=0), 0, 1).reshape(n_ex, -1)

    partial = partial_gram(shares)
    rows_out = partial.shape[2]
    everyone = ("param", "ex")
    received = lax.all_to_all(
        partial.reshape(n_param * n_group, rows_out, LANES), everyone, split_axis=0, concat_axis=0
    )
    tile, strip = sum_tiles(received)
    onward = [
        (p * n_group + e, p * n_group + (e + p + 1) % n_group) for p in range(n_param) for e in range(n_group)
    ]
    turned = lax.ppermute(tile[1], everyone, onward)
    message = jnp.concatenate([jnp.concatenate([tile[0], turned], axis=1), strip], axis=0)
    spread = lax.all_to_all(
        jnp.broadcast_to(message[None], (n_param,) + message.shape), "param", split_axis=0, concat_axis=0
    )
    gram = place_tiles(spread, lax.axis_index("ex"), n_ex, n_group)
    return (whole_features, gram)


def solution(mesh):
    return jax.shard_map(
        body,
        mesh=mesh,
        in_specs=(
            P("ex", None, "param"),
            P("ex", None, None),
            P("ex", None),
            P(None, "param"),
            P(),
        ),
        out_specs=(P("ex", "param"), P("ex", None)),
        check_vma=False,
    )
```

```python
import functools
import math

import jax
import jax.numpy as jnp
import ml_dtypes
import numpy as np
from jax import lax
from jax.experimental import pallas as pl
from jax.experimental.pallas import tpu as pltpu
from jax.sharding import PartitionSpec as P

D = 8192
SLAB = 64
TOKS = 128
K = 32768
LANES = 128
ROW_COST = 10_000_000
STEP_EX = 8
TAP = 256


def walsh_table(order):
    table = np.ones((1, 1), np.float32)
    while table.shape[0] < order:
        table = np.block([[table, table], [table, -table]])
    return table.astype(ml_dtypes.bfloat16)


def butterfly(parts):
    count = len(parts)
    half = 1
    while half < count:
        out = list(parts)
        for index in range(count):
            if not index & half:
                out[index] = parts[index] + parts[index | half]
                out[index | half] = parts[index] - parts[index | half]
        parts = out
        half *= 2
    return parts


def table_kernel(n_ex, width, acts_ref, cots_ref, ids_ref, signs_ref, walsh_ref, table_ref, grad_ref, flip_ref):
    step = pl.program_id(0)
    tiles = width // LANES
    rows = SLAB

    @pl.when(step == 0)
    def _():
        factor = 1.0 / math.sqrt(TOKS) / math.sqrt(SLAB * D)
        flip_ref[...] = signs_ref[...].astype(jnp.float32) * factor

    @pl.loop(0, STEP_EX)
    def _(i):
        e = step * STEP_EX + i
        live = (ids_ref[pl.ds(i, 1), :] != 0).astype(jnp.bfloat16)
        g = jnp.dot(cots_ref[i] * live, acts_ref[i], preferred_element_type=jnp.float32)
        g = g * flip_ref[...]
        for low in range(2):
            tile = [g[:, (2 * q + low) * LANES:(2 * q + low + 1) * LANES] for q in range(tiles // 2)]
            tile = butterfly(tile)
            for q in range(tiles // 2):
                parts = butterfly([tile[q][8 * s:8 * s + 8] for s in range(rows // 8)])
                for s in range(rows // 8):
                    grad_ref[2 * q + low, pl.ds(e * rows + 8 * s, 8), :] = parts[s]

    @pl.when(step == pl.num_programs(0) - 1)
    def _():
        lane = lax.broadcasted_iota(jnp.int32, (TAP, LANES), 1)
        low_half = jnp.where(lane < LANES // 2, 1.0, -1.0).astype(jnp.float32)

        @pl.loop(0, (rows // 8) * (tiles // 2))
        def _(index):
            s = index // (tiles // 2)
            q = index % (tiles // 2)
            high, low = [], []
            for r in range(8):
                pieces = [
                    grad_ref.at[2 * q + j][pl.ds(s * 8 + r, n_ex, stride=rows), :] for j in range(2)
                ]
                x = jnp.concatenate(pieces, axis=1)
                h = x.astype(jnp.bfloat16)
                high.append(h)
                low.append((x - h.astype(jnp.float32)).astype(jnp.bfloat16))
            nt = (((1,), (1,)), ((), ()))
            mixed = lax.dot_general(walsh_ref[...], jnp.concatenate(high, axis=0), nt, preferred_element_type=jnp.float32)
            mixed += lax.dot_general(walsh_ref[...], jnp.concatenate(low, axis=0), nt, preferred_element_type=jnp.float32)
            parts = butterfly([mixed[:, j * LANES:(j + 1) * LANES] for j in range(4)])
            for j in range(4):
                v = parts[j]
                v = v * low_half + pltpu.roll(v, LANES // 2, 1)
                table_ref[pl.ds((s * 4 + j) * width + q * TAP, TAP), :] = v


def gather_kernel(segments, start, rows_ref, table_ref, half_ref, sign_ref, *refs):
    n_extra = sum(extra is not None for _, _, extra in segments)
    extras, out_ref, bufs = refs[:n_extra], refs[-3], refs[-2:]
    n_block = segments[-1][1]

    def fetch(block, slot):
        base = pl.multiple_of(block * LANES, LANES)
        for j in range(LANES):
            bufs[slot][j:j + 1, :] = table_ref[pl.ds(rows_ref[base + j], 1), :]

    def finish(block, t, extra, first):
        here = pl.ds(start + block, 1)
        picked = jnp.where(half_ref[here, :] > 0, t[LANES // 2:], t[:LANES // 2]) * sign_ref[here, :]
        out_ref[block] = picked if extra is None else picked + extras[extra][block - first]

    fetch(0, 0)
    for first, last, extra in segments:

        @pl.loop(first // 2, last // 2)
        def _(i):
            t = bufs[0][...].T
            fetch(2 * i + 1, 1)
            finish(2 * i, t, extra, first)
            t = bufs[1][...].T
            fetch(jnp.minimum(2 * i + 2, n_block - 1), 0)
            finish(2 * i + 1, t, extra, first)


def whole(shape):
    return pl.BlockSpec(shape, lambda i, *_: (0,) * len(shape))


def make_table(activations, cotangents, token_ids, signs):
    n_ex, toks, width = activations.shape
    slab = cotangents.shape[2]
    return pl.pallas_call(
        functools.partial(table_kernel, n_ex, width),
        out_shape=pltpu.VMEM((slab // 2 * width, LANES), jnp.float32),
        grid=(n_ex // STEP_EX,),
        in_specs=[
            pl.BlockSpec((STEP_EX, toks, width), lambda i: (i, 0, 0)),
            pl.BlockSpec((STEP_EX, slab, toks), lambda i: (i, 0, 0)),
            pl.BlockSpec((STEP_EX, toks), lambda i: (i, 0)),
            whole((slab, width)),
            whole((TAP, TAP)),
        ],
        out_specs=pl.BlockSpec(memory_space=pltpu.VMEM),
        scratch_shapes=[
            pltpu.VMEM((width // LANES, n_ex * slab, LANES), jnp.float32),
            pltpu.VMEM((slab, width), jnp.float32),
        ],
        compiler_params=pltpu.CompilerParams(
            dimension_semantics=("arbitrary",), vmem_limit_bytes=30 * 1024 * 1024
        ),
        name="make_table",
    )(activations, jnp.swapaxes(cotangents, 1, 2), token_ids, signs, jnp.asarray(walsh_table(TAP)))


def gather_rows(table, index, core, first, count, after=(), add=()):
    half, sign = index[:2]
    rows = index[2 + core * 3 + max(first - 1, 0)]
    unit = half.shape[0] // 8
    n_block = count * unit
    start = (core * 4 + first) * unit
    segments, at = [], 0
    for number, (low, high, _) in enumerate(add):
        if at < low:
            segments.append((at, low, None))
        segments.append((low, high, number))
        at = high
    if at < n_block:
        segments.append((at, n_block, None))
    vmem = pl.BlockSpec(memory_space=pltpu.VMEM)
    n_add = len(add)

    def kernel(*refs):
        gather_kernel(segments, start, *refs[:4 + n_add], *refs[4 + n_add + len(after):])

    return pl.pallas_call(
        kernel,
        out_shape=jax.ShapeDtypeStruct((n_block, LANES // 2, LANES), jnp.float32),
        in_specs=[pl.BlockSpec(memory_space=pltpu.SMEM)] + [vmem] * (3 + n_add) + [pl.BlockSpec(memory_space=pl.ANY)] * len(after),
        out_specs=vmem,
        scratch_shapes=[pltpu.VMEM((LANES, LANES), jnp.float32)] * 2,
        compiler_params=pltpu.CompilerParams(vmem_limit_bytes=4 * 1024 * 1024),
        cost_estimate=pl.CostEstimate(
            flops=n_block * LANES * ROW_COST, bytes_accessed=n_block * LANES * 4096, transcendentals=0
        ),
        name="gather_rows",
    )(rows.reshape(-1), table, half, sign, *[x for _, _, x in add], *after)


STEPS = (1, 3, 2, 0)


def index_kernel(width, bits, me_ref, select_ref, half_ref, sign_ref, *rows_refs):
    me = me_ref[0]
    n_y, _, n_block, _ = select_ref.shape
    col_bits, width_bits = D.bit_length() - 1, width.bit_length() - 1
    for core in range(2):
        owner_core = (me & 1) ^ (1 - core)
        for place, step in enumerate(STEPS):
            chosen = select_ref[((me >> 1) + step) & (n_y - 1), owner_core]
            row = chosen >> col_bits
            column = chosen & (D - 1)
            shared = (column >> width_bits) & me
            parity = jnp.zeros_like(shared)
            for bit in range(bits):
                parity = parity ^ (shared >> bit & 1)
            here = pl.ds((core * n_y + place) * n_block, n_block)
            rows_ref, first = rows_refs[core * 3 + max(place - 1, 0)], (place == 1) * n_block
            rows_ref[first:first + n_block, :] = (row >> 1) * width + (column & (width - 1))
            half_ref[here, :] = row & 1
            sign_ref[here, :] = (1 - 2 * parity).astype(jnp.float32)


def make_index(select, me, n_param, width):
    n_block = select.shape[0] // LANES
    vmem = pl.BlockSpec(memory_space=pltpu.VMEM)
    return pl.pallas_call(
        functools.partial(index_kernel, width, n_param.bit_length() - 1),
        out_shape=(
            jax.ShapeDtypeStruct((n_block, LANES), jnp.int32),
            jax.ShapeDtypeStruct((n_block, LANES), jnp.float32),
        ) + tuple(jax.ShapeDtypeStruct((n * n_block // n_param, LANES), jnp.int32) for n in (2, 1, 1)) * 2,
        in_specs=[pl.BlockSpec(memory_space=pltpu.SMEM), vmem],
        out_specs=(vmem,) * 8,
        name="make_index",
    )(me.reshape(1), select.reshape(n_param // 2, 2, n_block // n_param, LANES))


def gram_kernel(n_ex, *refs):
    x_ref, out_ref, high_ref, low_ref = refs
    blocks = x_ref.shape[0]
    for b in range(blocks):
        x = jnp.concatenate([x_ref[b, j] for j in range(x_ref.shape[1])], axis=1)
        h = x.astype(jnp.bfloat16)
        low = (x - h.astype(jnp.float32)).astype(jnp.bfloat16)
        for at in ((b, b + blocks) if b < 10 else (b,)):
            high_ref[at * n_ex:(at + 1) * n_ex, :] = h
            low_ref[at * n_ex:(at + 1) * n_ex, :] = low
    half = LANES // 2
    left = lax.broadcasted_iota(jnp.int32, (n_ex // 2, LANES), 1) < half
    nt = (((1,), (1,)), ((), ()))

    @pl.loop(0, blocks)
    def _(b):
        first = pl.multiple_of(b * n_ex, n_ex)
        mine = pl.ds(first, n_ex)
        near = pl.ds(first, 10 * n_ex)
        t = lax.dot_general(high_ref[mine, :], high_ref[near, :], nt, preferred_element_type=jnp.float32)
        t += lax.dot_general(high_ref[mine, :], low_ref[near, :], nt, preferred_element_type=jnp.float32)
        t += lax.dot_general(low_ref[mine, :], high_ref[near, :], nt, preferred_element_type=jnp.float32)
        for p in range(8):
            q = (p + 1) // 2
            top = t[:n_ex // 2, q * LANES:(q + 1) * LANES]
            low = t[n_ex // 2:, q * LANES:(q + 1) * LANES]
            if p % 2:
                low = pltpu.roll(low, half, 1)
            else:
                top = pltpu.roll(top, half, 1)
            out_ref[p, b, :n_ex // 2, :] = jnp.where(left, top, low)
            out_ref[p, b, n_ex // 2:, :] = t[8 * p:8 * p + 8, :LANES]


def partial_gram(share):
    blocks, lane_tiles, n_ex, _ = share.shape
    width = lane_tiles * LANES
    vmem = pl.BlockSpec(memory_space=pltpu.VMEM)
    return pl.pallas_call(
        functools.partial(gram_kernel, n_ex),
        out_shape=jax.ShapeDtypeStruct((8, blocks, n_ex // 2 + 8, LANES), jnp.float32),
        in_specs=[vmem],
        out_specs=vmem,
        scratch_shapes=[pltpu.VMEM(((blocks + 10) * n_ex, width), jnp.bfloat16)] * 2,
        compiler_params=pltpu.CompilerParams(vmem_limit_bytes=16 * 1024 * 1024),
        name="partial_gram",
    )(share)


def sum_kernel(scale, x_ref, tile_ref, strip_ref):
    half = LANES // 2
    total = jnp.sum(x_ref[...], axis=0) * scale
    pair = total[:half // 2]
    tile = jnp.concatenate([pair[:, :half], pair[:, half:]], axis=0)
    tile_ref[0] = tile
    tile_ref[1] = tile.T
    strip_ref[...] = total[half // 2:]


def sum_tiles(received):
    vmem = pl.BlockSpec(memory_space=pltpu.VMEM)
    return pl.pallas_call(
        functools.partial(sum_kernel, 1.0 / K),
        out_shape=(
            jax.ShapeDtypeStruct((2, LANES // 2, LANES // 2), jnp.float32),
            jax.ShapeDtypeStruct((8, LANES), jnp.float32),
        ),
        in_specs=[vmem],
        out_specs=(vmem, vmem),
        compiler_params=pltpu.CompilerParams(vmem_limit_bytes=16 * 1024 * 1024),
        name="sum_tiles",
    )(received)


def place_kernel(me_ref, x_ref, out_ref):
    half = LANES // 2
    count = out_ref.shape[1] // half
    columns = [None] * count
    columns[0] = jnp.concatenate([x_ref[p, half:, :half] for p in range(8)], axis=0)
    for p in range(8):
        columns[p + 1] = x_ref[p, :half, :half]
        if count - 1 - p > p + 1:
            columns[count - 1 - p] = x_ref[p, :half, half:]
    row = jnp.concatenate(columns, axis=1)
    out_ref[...] = pltpu.roll(row, me_ref[0] * half, 1)


def place_tiles(tiles, me, n_ex, count):
    vmem = pl.BlockSpec(memory_space=pltpu.VMEM)
    return pl.pallas_call(
        place_kernel,
        out_shape=jax.ShapeDtypeStruct((n_ex, count * n_ex), jnp.float32),
        in_specs=[pl.BlockSpec(memory_space=pltpu.SMEM), vmem],
        out_specs=vmem,
        name="place_tiles",
    )(me.reshape(1), tiles)


def body(activations, cotangents, token_ids, signs, select):
    n_param, n_group = lax.axis_size("param"), lax.axis_size("ex")
    n_ex, _, width = activations.shape
    me = lax.axis_index("param")
    table = make_table(activations, cotangents, token_ids, signs)
    index = make_index(select, me, n_param, width)
    n_block = select.shape[0] // n_param // LANES
    swap = [(i, i ^ 1) for i in range(n_param)]

    def along(step):
        return [(i, (i + 2 * step) % n_param) for i in range(n_param)]

    mid = n_block // 2
    sent = gather_rows(table, index, 0, 2, 1)
    arrived = lax.ppermute(sent, "param", swap)
    far = gather_rows(table, index, 1, 2, 1, after=(sent,)) + arrived
    up = lax.ppermute(far[:mid], "param", along(1))
    down = lax.ppermute(far[mid:], "param", along(-1))
    sent = gather_rows(table, index, 0, 0, 2, after=(far,))
    arrived = lax.ppermute(sent, "param", swap)
    near = gather_rows(
        table, index, 1, 0, 2, after=(sent,), add=((0, mid, up), (n_block + mid, 2 * n_block, down))
    )
    outward = near[:n_block] + arrived[:n_block]
    from_below = lax.ppermute(outward, "param", along(1))
    inward = near[n_block:] + arrived[n_block:]
    from_above = lax.ppermute(inward, "param", along(-1))
    sent = gather_rows(table, index, 0, 3, 1, after=(outward, inward))
    arrived = lax.ppermute(sent, "param", swap)
    own = gather_rows(table, index, 1, 3, 1, after=(sent,))
    features = own + arrived + from_below + from_above
    share = lax.all_to_all(
        features.reshape(n_group, n_block // n_group, n_ex, LANES), "ex", split_axis=0, concat_axis=0
    )
    whole_features = jnp.swapaxes(features, 0, 1).reshape(n_ex, -1)

    partial = partial_gram(share)
    rows_out = partial.shape[2]
    everyone = ("param", "ex")
    received = lax.all_to_all(
        partial.reshape(n_param * n_group, rows_out, LANES), everyone, split_axis=0, concat_axis=0
    )
    tile, strip = sum_tiles(received)
    onward = [
        (p * n_group + e, p * n_group + (e + p + 1) % n_group) for p in range(n_param) for e in range(n_group)
    ]
    turned = lax.ppermute(tile[1], everyone, onward)
    message = jnp.concatenate([jnp.concatenate([tile[0], turned], axis=1), strip], axis=0)
    spread = lax.all_to_all(
        jnp.broadcast_to(message[None], (n_param,) + message.shape), "param", split_axis=0, concat_axis=0
    )
    gram = place_tiles(spread, lax.axis_index("ex"), n_ex, n_group)
    return (whole_features, gram)


def solution(mesh):
    return jax.shard_map(
        body,
        mesh=mesh,
        in_specs=(
            P("ex", None, "param"),
            P("ex", None, None),
            P("ex", None),
            P(None, "param"),
            P(),
        ),
        out_specs=(P("ex", "param"), P("ex", None)),
        check_vma=False,
    )
```

```python
import functools
import math

import jax
import jax.numpy as jnp
import ml_dtypes
import numpy as np
from jax import lax
from jax.experimental import pallas as pl
from jax.experimental.pallas import tpu as pltpu
from jax.sharding import PartitionSpec as P

D = 8192
SLAB = 64
TOKS = 128
K = 32768
LANES = 128
ROW_COST = 1_000_000_000
STEP_EX = 8
TAP = 256


def walsh_table(order):
    table = np.ones((1, 1), np.float32)
    while table.shape[0] < order:
        table = np.block([[table, table], [table, -table]])
    return table.astype(ml_dtypes.bfloat16)


def butterfly(parts):
    count = len(parts)
    half = 1
    while half < count:
        out = list(parts)
        for index in range(count):
            if not index & half:
                out[index] = parts[index] + parts[index | half]
                out[index | half] = parts[index] - parts[index | half]
        parts = out
        half *= 2
    return parts


def table_kernel(n_ex, width, acts_ref, cots_ref, ids_ref, signs_ref, walsh_ref, table_ref, grad_ref, flip_ref):
    step = pl.program_id(0)
    tiles = width // LANES
    rows = SLAB

    @pl.when(step == 0)
    def _():
        factor = 1.0 / math.sqrt(TOKS) / math.sqrt(SLAB * D)
        flip_ref[...] = signs_ref[...].astype(jnp.float32) * factor

    @pl.loop(0, STEP_EX)
    def _(i):
        e = step * STEP_EX + i
        live = (ids_ref[pl.ds(i, 1), :] != 0).astype(jnp.bfloat16)
        g = jnp.dot(cots_ref[i] * live, acts_ref[i], preferred_element_type=jnp.float32)
        g = g * flip_ref[...]
        for low in range(2):
            tile = [g[:, (2 * q + low) * LANES:(2 * q + low + 1) * LANES] for q in range(tiles // 2)]
            tile = butterfly(tile)
            for q in range(tiles // 2):
                parts = butterfly([tile[q][8 * s:8 * s + 8] for s in range(rows // 8)])
                for s in range(rows // 8):
                    grad_ref[2 * q + low, pl.ds(e * rows + 8 * s, 8), :] = parts[s]

    @pl.when(step == pl.num_programs(0) - 1)
    def _():
        lane = lax.broadcasted_iota(jnp.int32, (TAP, LANES), 1)
        low_half = jnp.where(lane < LANES // 2, 1.0, -1.0).astype(jnp.float32)

        @pl.loop(0, (rows // 8) * (tiles // 2))
        def _(index):
            s = index // (tiles // 2)
            q = index % (tiles // 2)
            high, low = [], []
            for r in range(8):
                pieces = [
                    grad_ref.at[2 * q + j][pl.ds(s * 8 + r, n_ex, stride=rows), :] for j in range(2)
                ]
                x = jnp.concatenate(pieces, axis=1)
                h = x.astype(jnp.bfloat16)
                high.append(h)
                low.append((x - h.astype(jnp.float32)).astype(jnp.bfloat16))
            nt = (((1,), (1,)), ((), ()))
            mixed = lax.dot_general(walsh_ref[...], jnp.concatenate(high, axis=0), nt, preferred_element_type=jnp.float32)
            mixed += lax.dot_general(walsh_ref[...], jnp.concatenate(low, axis=0), nt, preferred_element_type=jnp.float32)
            parts = butterfly([mixed[:, j * LANES:(j + 1) * LANES] for j in range(4)])
            for j in range(4):
                v = parts[j]
                v = v * low_half + pltpu.roll(v, LANES // 2, 1)
                table_ref[pl.ds((s * 4 + j) * width + q * TAP, TAP), :] = v


def gather_kernel(segments, start, rows_ref, table_ref, half_ref, sign_ref, *refs):
    n_extra = sum(extra is not None for _, _, extra in segments)
    extras, out_ref, bufs = refs[:n_extra], refs[-3], refs[-2:]
    n_block = segments[-1][1]

    def fetch(block, slot):
        base = pl.multiple_of(block * LANES, LANES)
        for j in range(LANES):
            bufs[slot][j:j + 1, :] = table_ref[pl.ds(rows_ref[base + j], 1), :]

    def finish(block, t, extra, first):
        here = pl.ds(start + block, 1)
        picked = jnp.where(half_ref[here, :] > 0, t[LANES // 2:], t[:LANES // 2]) * sign_ref[here, :]
        out_ref[block] = picked if extra is None else picked + extras[extra][block - first]

    fetch(0, 0)
    for first, last, extra in segments:

        @pl.loop(first // 2, last // 2)
        def _(i):
            t = bufs[0][...].T
            fetch(2 * i + 1, 1)
            finish(2 * i, t, extra, first)
            t = bufs[1][...].T
            fetch(jnp.minimum(2 * i + 2, n_block - 1), 0)
            finish(2 * i + 1, t, extra, first)


def whole(shape):
    return pl.BlockSpec(shape, lambda i, *_: (0,) * len(shape))


def make_table(activations, cotangents, token_ids, signs):
    n_ex, toks, width = activations.shape
    slab = cotangents.shape[2]
    return pl.pallas_call(
        functools.partial(table_kernel, n_ex, width),
        out_shape=pltpu.VMEM((slab // 2 * width, LANES), jnp.float32),
        grid=(n_ex // STEP_EX,),
        in_specs=[
            pl.BlockSpec((STEP_EX, toks, width), lambda i: (i, 0, 0)),
            pl.BlockSpec((STEP_EX, slab, toks), lambda i: (i, 0, 0)),
            pl.BlockSpec((STEP_EX, toks), lambda i: (i, 0)),
            whole((slab, width)),
            whole((TAP, TAP)),
        ],
        out_specs=pl.BlockSpec(memory_space=pltpu.VMEM),
        scratch_shapes=[
            pltpu.VMEM((width // LANES, n_ex * slab, LANES), jnp.float32),
            pltpu.VMEM((slab, width), jnp.float32),
        ],
        compiler_params=pltpu.CompilerParams(
            dimension_semantics=("arbitrary",), vmem_limit_bytes=46 * 1024 * 1024
        ),
        name="make_table",
    )(activations, jnp.swapaxes(cotangents, 1, 2), token_ids, signs, jnp.asarray(walsh_table(TAP)))


def gather_rows(table, index, core, group, after=(), add=()):
    half, sign = index[:2]
    rows = index[2 + core * len(GROUPS) + group]
    n_block = rows.shape[0]
    start = (core * len(GROUPS) + group) * n_block
    segments, at = [], 0
    for number, (low, high, _) in enumerate(add):
        if at < low:
            segments.append((at, low, None))
        segments.append((low, high, number))
        at = high
    if at < n_block:
        segments.append((at, n_block, None))
    vmem = pl.BlockSpec(memory_space=pltpu.VMEM)
    n_add = len(add)

    def kernel(*refs):
        gather_kernel(segments, start, *refs[:4 + n_add], *refs[4 + n_add + len(after):])

    return pl.pallas_call(
        kernel,
        out_shape=jax.ShapeDtypeStruct((n_block, LANES // 2, LANES), jnp.float32),
        in_specs=[pl.BlockSpec(memory_space=pltpu.SMEM)] + [vmem] * (3 + n_add) + [pl.BlockSpec(memory_space=pl.ANY)] * len(after),
        out_specs=vmem,
        scratch_shapes=[pltpu.VMEM((LANES, LANES), jnp.float32)] * 2,
        compiler_params=pltpu.CompilerParams(vmem_limit_bytes=4 * 1024 * 1024),
        cost_estimate=pl.CostEstimate(
            flops=n_block * LANES * ROW_COST, bytes_accessed=n_block * LANES * 4096, transcendentals=0
        ),
        name="gather_rows",
    )(rows.reshape(-1), table, half, sign, *[x for _, _, x in add], *after)


GROUPS = (((2, 0), (2, 1)), ((1, 0), (3, 0)), ((1, 1), (3, 1)), ((0, 0), (0, 1)))
FAR, FIRST, SECOND, OWN = range(4)


def index_kernel(width, bits, me_ref, select_ref, half_ref, sign_ref, *rows_refs):
    me = me_ref[0]
    n_y, _, n_block, _ = select_ref.shape
    mid = n_block // 2
    col_bits, width_bits = D.bit_length() - 1, width.bit_length() - 1
    for core in range(2):
        owner_core = (me & 1) ^ (1 - core)
        for group, pieces in enumerate(GROUPS):
            for place, (step, part) in enumerate(pieces):
                chosen = select_ref[((me >> 1) + step) & (n_y - 1), owner_core, part * mid:(part + 1) * mid, :]
                row = chosen >> col_bits
                column = chosen & (D - 1)
                shared = (column >> width_bits) & me
                parity = jnp.zeros_like(shared)
                for bit in range(bits):
                    parity = parity ^ (shared >> bit & 1)
                here = pl.ds((core * len(GROUPS) + group) * n_block + place * mid, mid)
                rows = (row >> 1) * width + (column & (width - 1))
                rows_refs[core * len(GROUPS) + group][place * mid:(place + 1) * mid, :] = rows
                half_ref[here, :] = row & 1
                sign_ref[here, :] = (1 - 2 * parity).astype(jnp.float32)


def make_index(select, me, n_param, width):
    n_block = select.shape[0] // LANES
    vmem = pl.BlockSpec(memory_space=pltpu.VMEM)
    return pl.pallas_call(
        functools.partial(index_kernel, width, n_param.bit_length() - 1),
        out_shape=(
            jax.ShapeDtypeStruct((n_block, LANES), jnp.int32),
            jax.ShapeDtypeStruct((n_block, LANES), jnp.float32),
        ) + (jax.ShapeDtypeStruct((n_block // n_param, LANES), jnp.int32),) * n_param,
        in_specs=[pl.BlockSpec(memory_space=pltpu.SMEM), vmem],
        out_specs=(vmem,) * (2 + n_param),
        name="make_index",
    )(me.reshape(1), select.reshape(n_param // 2, 2, n_block // n_param, LANES))


def gram_kernel(n_ex, core_ref, *refs):
    x_refs, out_ref, high_ref, low_ref, part_ref = refs[:-4], refs[-4], refs[-3], refs[-2], refs[-1]
    core = core_ref[0]
    blocks = x_refs[0].shape[0]
    half = LANES // 2
    for b in range(blocks):
        x = jnp.concatenate([r[b] for r in x_refs], axis=1)
        h = x.astype(jnp.bfloat16)
        low = (x - h.astype(jnp.float32)).astype(jnp.bfloat16)
        for at in ((b + 8, b - 8) if b >= 8 else (b + 8,)):
            high_ref[at * n_ex:(at + 1) * n_ex, :] = h
            low_ref[at * n_ex:(at + 1) * n_ex, :] = low
    left = lax.broadcasted_iota(jnp.int32, (n_ex // 2, LANES), 1) < half
    nt = (((1,), (1,)), ((), ()))

    @pl.loop(0, blocks // 4)
    def _(quad):
        rows = pl.ds(pl.multiple_of(quad * 4 * n_ex, 4 * n_ex), 12 * n_ex)
        columns = pl.ds(pl.multiple_of((quad * 4 + 8) * n_ex, 4 * n_ex), 4 * n_ex)
        t = lax.dot_general(high_ref[rows, :], high_ref[columns, :], nt, preferred_element_type=jnp.float32)
        t += lax.dot_general(high_ref[rows, :], low_ref[columns, :], nt, preferred_element_type=jnp.float32)
        t += lax.dot_general(low_ref[rows, :], high_ref[columns, :], nt, preferred_element_type=jnp.float32)
        part_ref[...] = t
        for v in range(4):
            lanes = slice(v // 2 * LANES, (v // 2 + 1) * LANES)
            for m in range(4):
                offset = 2 * m + core + 1
                first = pl.multiple_of((8 + v - offset) * n_ex, n_ex)
                top = part_ref[pl.ds(first, n_ex // 2), lanes]
                low = part_ref[pl.ds(first + n_ex // 2, n_ex // 2), lanes]
                strip = part_ref[pl.ds(pl.multiple_of((8 + v) * n_ex + 8 * (offset - 1), 8), 8), lanes]
                if v % 2:
                    top = pltpu.roll(top, half, 1)
                    strip = pltpu.roll(strip, half, 1)
                else:
                    low = pltpu.roll(low, half, 1)
                row_block = (quad * 4 + v + blocks - offset) & (blocks - 1)
                out_ref[m, row_block, :n_ex // 2, :] = jnp.where(left, top, low)
                out_ref[m, quad * 4 + v, n_ex // 2:, :] = strip


def partial_gram(shares, core):
    blocks, n_ex, _ = shares[0].shape
    width = len(shares) * LANES
    vmem = pl.BlockSpec(memory_space=pltpu.VMEM)
    return pl.pallas_call(
        functools.partial(gram_kernel, n_ex),
        out_shape=jax.ShapeDtypeStruct((4, blocks, n_ex // 2 + 8, LANES), jnp.float32),
        in_specs=[pl.BlockSpec(memory_space=pltpu.SMEM)] + [vmem] * len(shares),
        out_specs=vmem,
        scratch_shapes=[pltpu.VMEM(((blocks + 8) * n_ex, width), jnp.bfloat16)] * 2
        + [pltpu.VMEM((12 * n_ex, 4 * n_ex), jnp.float32)],
        compiler_params=pltpu.CompilerParams(vmem_limit_bytes=16 * 1024 * 1024),
        name="partial_gram",
    )(core.reshape(1), *shares)


def sum_kernel(scale, x_ref, tile_ref, strip_ref):
    half = LANES // 2
    total = jnp.sum(x_ref[...], axis=0) * scale
    pair = total[:half // 2]
    tile = jnp.concatenate([pair[:, :half], pair[:, half:]], axis=0)
    tile_ref[0] = tile
    tile_ref[1] = tile.T
    strip_ref[...] = total[half // 2:]


def sum_tiles(received):
    vmem = pl.BlockSpec(memory_space=pltpu.VMEM)
    return pl.pallas_call(
        functools.partial(sum_kernel, 1.0 / K),
        out_shape=(
            jax.ShapeDtypeStruct((2, LANES // 2, LANES // 2), jnp.float32),
            jax.ShapeDtypeStruct((8, LANES), jnp.float32),
        ),
        in_specs=[vmem],
        out_specs=(vmem, vmem),
        compiler_params=pltpu.CompilerParams(vmem_limit_bytes=16 * 1024 * 1024),
        name="sum_tiles",
    )(received)


def place_kernel(me_ref, x_ref, out_ref):
    half = LANES // 2
    count = out_ref.shape[1] // half
    columns = [None] * count
    columns[0] = jnp.concatenate([x_ref[p, half:, :half] for p in range(8)], axis=0)
    for p in range(8):
        columns[p + 1] = x_ref[p, :half, :half]
        if count - 1 - p > p + 1:
            columns[count - 1 - p] = x_ref[p, :half, half:]
    row = jnp.concatenate(columns, axis=1)
    out_ref[...] = pltpu.roll(row, me_ref[0] * half, 1)


def place_tiles(tiles, me, n_ex, count):
    vmem = pl.BlockSpec(memory_space=pltpu.VMEM)
    return pl.pallas_call(
        place_kernel,
        out_shape=jax.ShapeDtypeStruct((n_ex, count * n_ex), jnp.float32),
        in_specs=[pl.BlockSpec(memory_space=pltpu.SMEM), vmem],
        out_specs=vmem,
        name="place_tiles",
    )(me.reshape(1), tiles)


def body(activations, cotangents, token_ids, signs, select):
    n_param, n_group = lax.axis_size("param"), lax.axis_size("ex")
    n_ex, _, width = activations.shape
    me = lax.axis_index("param")
    table = make_table(activations, cotangents, token_ids, signs)
    index = make_index(select, me, n_param, width)
    n_block = select.shape[0] // n_param // LANES
    n_y = n_param // 2
    swap = [(i, i ^ 1) for i in range(n_param)]

    def along(step):
        return [(i, (i + 2 * step) % n_param) for i in range(n_param)]

    mid = n_block // 2
    sent = gather_rows(table, index, 0, FAR)
    arrived = lax.ppermute(sent, "param", swap)
    far = gather_rows(table, index, 1, FAR, after=(sent,))
    outward = (far[:mid] + arrived[:mid], far[mid:] + arrived[mid:])
    up, down = lax.ppermute(outward[0], "param", along(1)), lax.ppermute(outward[1], "param", along(-1))
    sent_first = gather_rows(table, index, 0, FIRST, after=outward)
    arrived_first = lax.ppermute(sent_first, "param", swap)
    sent_second = gather_rows(table, index, 0, SECOND, after=(sent_first,))
    arrived_second = lax.ppermute(sent_second, "param", swap)
    first = gather_rows(table, index, 1, FIRST, after=(sent_second,), add=((0, mid, up),))
    outward = (first[:mid] + arrived_first[:mid], first[mid:] + arrived_first[mid:])
    first = lax.ppermute(outward[0], "param", along(1)), lax.ppermute(outward[1], "param", along(-1))
    second = gather_rows(table, index, 1, SECOND, after=outward, add=((mid, n_block, down),))
    outward = (second[:mid] + arrived_second[:mid], second[mid:] + arrived_second[mid:])
    second = lax.ppermute(outward[0], "param", along(1)), lax.ppermute(outward[1], "param", along(-1))
    sent = gather_rows(table, index, 0, OWN, after=outward)
    arrived = lax.ppermute(sent, "param", swap)
    own = gather_rows(table, index, 1, OWN, after=(sent,))
    front = own[:mid] + arrived[:mid] + first[0] + first[1]
    own, arrived, front = lax.optimization_barrier((own, arrived, front))
    back = own[mid:] + arrived[mid:] + second[0] + second[1]
    features = (front, back)
    shares = [lax.all_to_all(x, "ex", split_axis=0, concat_axis=0) for x in features]
    shares += [lax.ppermute(x, "param", swap) for x in shares]
    whole_features = jnp.swapaxes(jnp.concatenate(features, axis=0), 0, 1).reshape(n_ex, -1)

    partial = partial_gram(shares, me % 2)
    rows_out = partial.shape[2]
    everyone = ("param", "ex")
    alike = [
        [(2 * y + core) * n_group + e for y in range(n_y) for e in range(n_group)] for core in range(2)
    ]
    received = lax.all_to_all(
        partial.reshape(n_y * n_group, rows_out, LANES),
        everyone,
        split_axis=0,
        concat_axis=0,
        axis_index_groups=alike,
    )
    tile, strip = sum_tiles(received)
    onward = [
        (p * n_group + e, p * n_group + (e + p + 1) % n_group) for p in range(n_param) for e in range(n_group)
    ]
    turned = lax.ppermute(tile[1], everyone, onward)
    message = jnp.concatenate([jnp.concatenate([tile[0], turned], axis=1), strip], axis=0)
    spread = lax.all_to_all(
        jnp.broadcast_to(message[None], (n_param,) + message.shape), "param", split_axis=0, concat_axis=0
    )
    gram = place_tiles(spread, lax.axis_index("ex"), n_ex, n_group)
    return (whole_features, gram)


def solution(mesh):
    return jax.shard_map(
        body,
        mesh=mesh,
        in_specs=(
            P("ex", None, "param"),
            P("ex", None, None),
            P("ex", None),
            P(None, "param"),
            P(),
        ),
        out_specs=(P("ex", "param"), P("ex", None)),
        check_vma=False,
    )
```

```python
import functools
import math

import jax
import jax.numpy as jnp
import ml_dtypes
import numpy as np
from jax import lax
from jax.experimental import pallas as pl
from jax.experimental.pallas import tpu as pltpu
from jax.sharding import PartitionSpec as P

D = 8192
SLAB = 64
TOKS = 128
K = 32768
LANES = 128
ROW_COST = 10_000_000
STEP_EX = 8
TAP = 256
EXTRA_ROWS = 8


def walsh_table(order):
    table = np.ones((1, 1), np.float32)
    while table.shape[0] < order:
        table = np.block([[table, table], [table, -table]])
    return table.astype(ml_dtypes.bfloat16)


def butterfly(parts):
    count = len(parts)
    half = 1
    while half < count:
        out = list(parts)
        for index in range(count):
            if not index & half:
                out[index] = parts[index] + parts[index | half]
                out[index | half] = parts[index] - parts[index | half]
        parts = out
        half *= 2
    return parts


def table_kernel(n_ex, width, acts_ref, *refs):
    sources, (table_ref, grad_ref, flip_ref), copies, sems = refs[:4], refs[4:7], refs[7:11], refs[11]
    cots_ref, ids_ref, signs_ref, walsh_ref = copies
    step = pl.program_id(0)
    tiles = width // LANES
    rows = SLAB
    stride = SLAB + EXTRA_ROWS

    @pl.when(step == 0)
    def _():
        started = [pltpu.make_async_copy(a, b, sems.at[i]) for i, (a, b) in enumerate(zip(sources, copies))]
        for copy in started:
            copy.start()
        for copy in started:
            copy.wait()
        factor = 1.0 / math.sqrt(TOKS) / math.sqrt(SLAB * D)
        flip_ref[...] = signs_ref[...].astype(jnp.float32) * factor

    @pl.loop(0, STEP_EX, unroll=4)
    def _(i):
        e = step * STEP_EX + i
        live = (ids_ref[pl.ds(e, 1), :] != 0).astype(jnp.bfloat16)
        g = jnp.dot(cots_ref[e] * live, acts_ref[i], preferred_element_type=jnp.float32)
        g = g * flip_ref[...]
        for low in range(2):
            tile = [g[:, (2 * q + low) * LANES:(2 * q + low + 1) * LANES] for q in range(tiles // 2)]
            tile = butterfly(tile)
            for q in range(tiles // 2):
                parts = butterfly([tile[q][8 * s:8 * s + 8] for s in range(rows // 8)])
                for s in range(rows // 8):
                    grad_ref[2 * q + low, pl.ds(e * stride + 8 * s, 8), :] = parts[s]

    @pl.when(step == pl.num_programs(0) - 1)
    def _():
        lane = lax.broadcasted_iota(jnp.int32, (TAP, LANES), 1)
        low_half = jnp.where(lane < LANES // 2, 1.0, -1.0).astype(jnp.float32)

        @pl.loop(0, (rows // 8) * (tiles // 2), unroll=4)
        def _(index):
            s = index // (tiles // 2)
            q = index % (tiles // 2)
            high, low = [], []
            for r in range(8):
                pieces = [
                    grad_ref.at[2 * q + j][pl.ds(s * 8 + r, n_ex, stride=stride), :] for j in range(2)
                ]
                x = jnp.concatenate(pieces, axis=1)
                h = x.astype(jnp.bfloat16)
                high.append(h)
                low.append((x - h.astype(jnp.float32)).astype(jnp.bfloat16))
            nt = (((1,), (1,)), ((), ()))
            mixed = lax.dot_general(walsh_ref[...], jnp.concatenate(high, axis=0), nt, preferred_element_type=jnp.float32)
            mixed += lax.dot_general(walsh_ref[...], jnp.concatenate(low, axis=0), nt, preferred_element_type=jnp.float32)
            parts = butterfly([mixed[:, j * LANES:(j + 1) * LANES] for j in range(4)])
            for j in range(4):
                v = parts[j]
                v = v * low_half + pltpu.roll(v, LANES // 2, 1)
                table_ref[pl.ds((s * 4 + j) * width + q * TAP, TAP), :] = v


def gather_kernel(segments, start, rows_ref, table_ref, half_ref, sign_ref, *refs):
    n_extra = sum(extra is not None for _, _, extra in segments)
    extras, out_ref, bufs = refs[:n_extra], refs[-3], refs[-2:]
    n_block = segments[-1][1]

    def fetch(block, slot):
        base = pl.multiple_of(block * LANES, LANES)
        for j in range(LANES):
            bufs[slot][j:j + 1, :] = table_ref[pl.ds(rows_ref[base + j], 1), :]

    def finish(block, t, extra, first):
        here = pl.ds(start + block, 1)
        picked = jnp.where(half_ref[here, :] > 0, t[LANES // 2:], t[:LANES // 2]) * sign_ref[here, :]
        out_ref[block] = picked if extra is None else picked + extras[extra][block - first]

    fetch(0, 0)
    for first, last, extra in segments:

        @pl.loop(first // 2, last // 2)
        def _(i):
            t = bufs[0][...].T
            fetch(2 * i + 1, 1)
            finish(2 * i, t, extra, first)
            t = bufs[1][...].T
            fetch(jnp.minimum(2 * i + 2, n_block - 1), 0)
            finish(2 * i + 1, t, extra, first)


def whole(shape):
    return pl.BlockSpec(shape, lambda i, *_: (0,) * len(shape))


def make_table(activations, cotangents, token_ids, signs):
    n_ex, toks, width = activations.shape
    slab = cotangents.shape[2]
    return pl.pallas_call(
        functools.partial(table_kernel, n_ex, width),
        out_shape=pltpu.VMEM((slab // 2 * width, LANES), jnp.float32),
        grid=(n_ex // STEP_EX,),
        in_specs=[
            pl.BlockSpec((STEP_EX, toks, width), lambda i: (i, 0, 0)),
        ] + [pl.BlockSpec(memory_space=pltpu.HBM)] * 4,
        out_specs=pl.BlockSpec(memory_space=pltpu.VMEM),
        scratch_shapes=[
            pltpu.VMEM((width // LANES, n_ex * (slab + EXTRA_ROWS), LANES), jnp.float32),
            pltpu.VMEM((slab, width), jnp.float32),
            pltpu.VMEM((n_ex, slab, toks), cotangents.dtype),
            pltpu.VMEM(token_ids.shape, token_ids.dtype),
            pltpu.VMEM(signs.shape, signs.dtype),
            pltpu.VMEM((TAP, TAP), jnp.bfloat16),
            pltpu.SemaphoreType.DMA((4,)),
        ],
        compiler_params=pltpu.CompilerParams(
            dimension_semantics=("arbitrary",), vmem_limit_bytes=30 * 1024 * 1024
        ),
        cost_estimate=pl.CostEstimate(flops=10**13, bytes_accessed=2**25, transcendentals=0),
        name="make_table",
    )(activations, jnp.swapaxes(cotangents, 1, 2), token_ids, signs, jnp.asarray(walsh_table(TAP)))


def gather_rows(table, index, core, group, after=(), add=()):
    half, sign = index[:2]
    rows = index[2 + core * len(GROUPS) + group]
    n_block = rows.shape[0]
    start = (core * len(GROUPS) + group) * n_block
    segments, at = [], 0
    for number, (low, high, _) in enumerate(add):
        if at < low:
            segments.append((at, low, None))
        segments.append((low, high, number))
        at = high
    if at < n_block:
        segments.append((at, n_block, None))
    vmem = pl.BlockSpec(memory_space=pltpu.VMEM)
    n_add = len(add)

    def kernel(*refs):
        gather_kernel(segments, start, *refs[:4 + n_add], *refs[4 + n_add + len(after):])

    return pl.pallas_call(
        kernel,
        out_shape=jax.ShapeDtypeStruct((n_block, LANES // 2, LANES), jnp.float32),
        in_specs=[pl.BlockSpec(memory_space=pltpu.SMEM)] + [vmem] * (3 + n_add) + [pl.BlockSpec(memory_space=pl.ANY)] * len(after),
        out_specs=vmem,
        scratch_shapes=[pltpu.VMEM((LANES, LANES), jnp.float32)] * 2,
        compiler_params=pltpu.CompilerParams(vmem_limit_bytes=4 * 1024 * 1024),
        cost_estimate=pl.CostEstimate(
            flops=n_block * LANES * ROW_COST, bytes_accessed=n_block * LANES * 4096, transcendentals=0
        ),
        name="gather_rows",
    )(rows.reshape(-1), table, half, sign, *[x for _, _, x in add], *after)


GROUPS = (((2, 0), (2, 1)), ((1, 0), (3, 0)), ((1, 1), (3, 1)), ((0, 0), (0, 1)))
FAR, FIRST, SECOND, OWN = range(4)


def index_kernel(width, bits, me_ref, select_ref, half_ref, sign_ref, *rows_refs):
    me = me_ref[0]
    n_y, _, n_block, _ = select_ref.shape
    mid = n_block // 2
    col_bits, width_bits = D.bit_length() - 1, width.bit_length() - 1
    for core in range(2):
        owner_core = (me & 1) ^ (1 - core)
        for group, pieces in enumerate(GROUPS):
            for place, (step, part) in enumerate(pieces):
                chosen = select_ref[((me >> 1) + step) & (n_y - 1), owner_core, part * mid:(part + 1) * mid, :]
                row = chosen >> col_bits
                column = chosen & (D - 1)
                shared = (column >> width_bits) & me
                parity = jnp.zeros_like(shared)
                for bit in range(bits):
                    parity = parity ^ (shared >> bit & 1)
                here = pl.ds((core * len(GROUPS) + group) * n_block + place * mid, mid)
                rows = (row >> 1) * width + (column & (width - 1))
                rows_refs[core * len(GROUPS) + group][place * mid:(place + 1) * mid, :] = rows
                half_ref[here, :] = row & 1
                sign_ref[here, :] = (1 - 2 * parity).astype(jnp.float32)


def make_index(select, me, n_param, width):
    n_block = select.shape[0] // LANES
    vmem = pl.BlockSpec(memory_space=pltpu.VMEM)
    return pl.pallas_call(
        functools.partial(index_kernel, width, n_param.bit_length() - 1),
        out_shape=(
            jax.ShapeDtypeStruct((n_block, LANES), jnp.int32),
            jax.ShapeDtypeStruct((n_block, LANES), jnp.float32),
        ) + (jax.ShapeDtypeStruct((n_block // n_param, LANES), jnp.int32),) * n_param,
        in_specs=[pl.BlockSpec(memory_space=pltpu.SMEM), vmem],
        out_specs=(vmem,) * (2 + n_param),
        compiler_params=pltpu.CompilerParams(vmem_limit_bytes=4 * 1024 * 1024),
        name="make_index",
    )(me.reshape(1), select.reshape(n_param // 2, 2, n_block // n_param, LANES))


def gram_kernel(n_ex, core_ref, *refs):
    x_refs, out_ref, high_ref, low_ref, part_ref = refs[:-4], refs[-4], refs[-3], refs[-2], refs[-1]
    core = core_ref[0]
    blocks = x_refs[0].shape[0]
    half = LANES // 2
    for b in range(blocks):
        x = jnp.concatenate([r[b] for r in x_refs], axis=1)
        h = x.astype(jnp.bfloat16)
        low = (x - h.astype(jnp.float32)).astype(jnp.bfloat16)
        for at in ((b + 8, b - 8) if b >= 8 else (b + 8,)):
            high_ref[at * n_ex:(at + 1) * n_ex, :] = h
            low_ref[at * n_ex:(at + 1) * n_ex, :] = low
    left = lax.broadcasted_iota(jnp.int32, (n_ex // 2, LANES), 1) < half
    nt = (((1,), (1,)), ((), ()))

    @pl.loop(0, blocks // 4)
    def _(quad):
        rows = pl.ds(pl.multiple_of(quad * 4 * n_ex, 4 * n_ex), 12 * n_ex)
        columns = pl.ds(pl.multiple_of((quad * 4 + 8) * n_ex, 4 * n_ex), 4 * n_ex)
        t = lax.dot_general(high_ref[rows, :], high_ref[columns, :], nt, preferred_element_type=jnp.float32)
        t += lax.dot_general(high_ref[rows, :], low_ref[columns, :], nt, preferred_element_type=jnp.float32)
        t += lax.dot_general(low_ref[rows, :], high_ref[columns, :], nt, preferred_element_type=jnp.float32)
        part_ref[...] = t
        for v in range(4):
            lanes = slice(v // 2 * LANES, (v // 2 + 1) * LANES)
            for m in range(4):
                offset = 2 * m + core + 1
                first = pl.multiple_of((8 + v - offset) * n_ex, n_ex)
                top = part_ref[pl.ds(first, n_ex // 2), lanes]
                low = part_ref[pl.ds(first + n_ex // 2, n_ex // 2), lanes]
                strip = part_ref[pl.ds(pl.multiple_of((8 + v) * n_ex + 8 * (offset - 1), 8), 8), lanes]
                if v % 2:
                    top = pltpu.roll(top, half, 1)
                    strip = pltpu.roll(strip, half, 1)
                else:
                    low = pltpu.roll(low, half, 1)
                row_block = (quad * 4 + v + blocks - offset) & (blocks - 1)
                out_ref[m, row_block, :n_ex // 2, :] = jnp.where(left, top, low)
                out_ref[m, quad * 4 + v, n_ex // 2:, :] = strip


def partial_gram(shares, core):
    blocks, n_ex, _ = shares[0].shape
    width = len(shares) * LANES
    vmem = pl.BlockSpec(memory_space=pltpu.VMEM)
    return pl.pallas_call(
        functools.partial(gram_kernel, n_ex),
        out_shape=jax.ShapeDtypeStruct((4, blocks, n_ex // 2 + 8, LANES), jnp.float32),
        in_specs=[pl.BlockSpec(memory_space=pltpu.SMEM)] + [vmem] * len(shares),
        out_specs=vmem,
        scratch_shapes=[pltpu.VMEM(((blocks + 8) * n_ex, width), jnp.bfloat16)] * 2
        + [pltpu.VMEM((12 * n_ex, 4 * n_ex), jnp.float32)],
        compiler_params=pltpu.CompilerParams(vmem_limit_bytes=16 * 1024 * 1024),
        name="partial_gram",
    )(core.reshape(1), *shares)


def sum_kernel(scale, x_ref, tile_ref, strip_ref):
    half = LANES // 2
    total = jnp.sum(x_ref[...], axis=0) * scale
    pair = total[:half // 2]
    tile = jnp.concatenate([pair[:, :half], pair[:, half:]], axis=0)
    tile_ref[0] = tile
    tile_ref[1] = tile.T
    strip_ref[...] = total[half // 2:]


def sum_tiles(received):
    vmem = pl.BlockSpec(memory_space=pltpu.VMEM)
    return pl.pallas_call(
        functools.partial(sum_kernel, 1.0 / K),
        out_shape=(
            jax.ShapeDtypeStruct((2, LANES // 2, LANES // 2), jnp.float32),
            jax.ShapeDtypeStruct((8, LANES), jnp.float32),
        ),
        in_specs=[vmem],
        out_specs=(vmem, vmem),
        compiler_params=pltpu.CompilerParams(vmem_limit_bytes=4 * 1024 * 1024),
        name="sum_tiles",
    )(received)


def place_kernel(me_ref, x_ref, out_ref):
    half = LANES // 2
    count = out_ref.shape[1] // half
    columns = [None] * count
    columns[0] = jnp.concatenate([x_ref[p, half:, :half] for p in range(8)], axis=0)
    for p in range(8):
        columns[p + 1] = x_ref[p, :half, :half]
        if count - 1 - p > p + 1:
            columns[count - 1 - p] = x_ref[p, :half, half:]
    row = jnp.concatenate(columns, axis=1)
    out_ref[...] = pltpu.roll(row, me_ref[0] * half, 1)


def place_tiles(tiles, me, n_ex, count):
    vmem = pl.BlockSpec(memory_space=pltpu.VMEM)
    return pl.pallas_call(
        place_kernel,
        out_shape=jax.ShapeDtypeStruct((n_ex, count * n_ex), jnp.float32),
        in_specs=[pl.BlockSpec(memory_space=pltpu.SMEM), vmem],
        out_specs=vmem,
        compiler_params=pltpu.CompilerParams(vmem_limit_bytes=4 * 1024 * 1024),
        name="place_tiles",
    )(me.reshape(1), tiles)


def body(activations, cotangents, token_ids, signs, select):
    n_param, n_group = lax.axis_size("param"), lax.axis_size("ex")
    n_ex, _, width = activations.shape
    me = lax.axis_index("param")
    table = make_table(activations, cotangents, token_ids, signs)
    index = make_index(select, me, n_param, width)
    n_block = select.shape[0] // n_param // LANES
    n_y = n_param // 2
    swap = [(i, i ^ 1) for i in range(n_param)]

    def along(step):
        return [(i, (i + 2 * step) % n_param) for i in range(n_param)]

    mid = n_block // 2
    sent = gather_rows(table, index, 0, FAR)
    arrived = lax.ppermute(sent, "param", swap)
    far = gather_rows(table, index, 1, FAR, after=(sent,))
    outward = (far[:mid] + arrived[:mid], far[mid:] + arrived[mid:])
    up, down = lax.ppermute(outward[0], "param", along(1)), lax.ppermute(outward[1], "param", along(-1))
    sent_first = gather_rows(table, index, 0, FIRST, after=outward)
    arrived_first = lax.ppermute(sent_first, "param", swap)
    sent_second = gather_rows(table, index, 0, SECOND, after=(sent_first,))
    arrived_second = lax.ppermute(sent_second, "param", swap)
    first = gather_rows(table, index, 1, FIRST, after=(sent_second,), add=((0, mid, up),))
    outward = (first[:mid] + arrived_first[:mid], first[mid:] + arrived_first[mid:])
    first = lax.ppermute(outward[0], "param", along(1)), lax.ppermute(outward[1], "param", along(-1))
    second = gather_rows(table, index, 1, SECOND, after=outward, add=((mid, n_block, down),))
    outward = (second[:mid] + arrived_second[:mid], second[mid:] + arrived_second[mid:])
    second = lax.ppermute(outward[0], "param", along(1)), lax.ppermute(outward[1], "param", along(-1))
    sent = gather_rows(table, index, 0, OWN, after=outward)
    arrived = lax.ppermute(sent, "param", swap)
    own = gather_rows(table, index, 1, OWN, after=(sent,))
    front = own[:mid] + arrived[:mid] + first[0] + first[1]
    own, arrived, front = lax.optimization_barrier((own, arrived, front))
    back = own[mid:] + arrived[mid:] + second[0] + second[1]
    features = (front, back)
    shares = [lax.all_to_all(x, "ex", split_axis=0, concat_axis=0) for x in features]
    shares += [lax.ppermute(x, "param", swap) for x in shares]
    whole_features = jnp.swapaxes(jnp.concatenate(features, axis=0), 0, 1).reshape(n_ex, -1)

    partial = partial_gram(shares, me % 2)
    rows_out = partial.shape[2]
    everyone = ("param", "ex")
    alike = [
        [(2 * y + core) * n_group + e for y in range(n_y) for e in range(n_group)] for core in range(2)
    ]
    received = lax.all_to_all(
        partial.reshape(n_y * n_group, rows_out, LANES),
        everyone,
        split_axis=0,
        concat_axis=0,
        axis_index_groups=alike,
    )
    tile, strip = sum_tiles(received)
    onward = [
        (p * n_group + e, p * n_group + (e + p + 1) % n_group) for p in range(n_param) for e in range(n_group)
    ]
    turned = lax.ppermute(tile[1], everyone, onward)
    message = jnp.concatenate([jnp.concatenate([tile[0], turned], axis=1), strip], axis=0)
    spread = lax.all_to_all(
        jnp.broadcast_to(message[None], (n_param,) + message.shape), "param", split_axis=0, concat_axis=0
    )
    gram = place_tiles(spread, lax.axis_index("ex"), n_ex, n_group)
    return (whole_features, gram)


def solution(mesh):
    return jax.shard_map(
        body,
        mesh=mesh,
        in_specs=(
            P("ex", None, "param"),
            P("ex", None, None),
            P("ex", None),
            P(None, "param"),
            P(),
        ),
        out_specs=(P("ex", "param"), P("ex", None)),
        check_vma=False,
    )
```

```python
import functools
import math

import jax
import jax.numpy as jnp
import ml_dtypes
import numpy as np
from jax import lax
from jax.experimental import pallas as pl
from jax.experimental.pallas import tpu as pltpu
from jax.sharding import PartitionSpec as P

D = 8192
SLAB = 64
TOKS = 128
K = 32768
LANES = 128
ROW_COST = 10_000_000
STEP_EX = 8
TAP = 256
EXTRA_ROWS = 8


def walsh_table(order):
    table = np.ones((1, 1), np.float32)
    while table.shape[0] < order:
        table = np.block([[table, table], [table, -table]])
    return table.astype(ml_dtypes.bfloat16)


def butterfly(parts):
    count = len(parts)
    half = 1
    while half < count:
        out = list(parts)
        for index in range(count):
            if not index & half:
                out[index] = parts[index] + parts[index | half]
                out[index | half] = parts[index] - parts[index | half]
        parts = out
        half *= 2
    return parts


def table_kernel(n_ex, width, acts_ref, *refs):
    sources, (table_ref, grad_ref, flip_ref), copies, sems = refs[:4], refs[4:7], refs[7:11], refs[11]
    cots_ref, ids_ref, signs_ref, walsh_ref = copies
    step = pl.program_id(0)
    tiles = width // LANES
    rows = SLAB
    stride = SLAB + EXTRA_ROWS

    @pl.when(step == 0)
    def _():
        started = [pltpu.make_async_copy(a, b, sems.at[i]) for i, (a, b) in enumerate(zip(sources, copies))]
        for copy in started:
            copy.start()
        for copy in started:
            copy.wait()
        factor = 1.0 / math.sqrt(TOKS) / math.sqrt(SLAB * D)
        flip_ref[...] = signs_ref[...].astype(jnp.float32) * factor

    @pl.loop(0, STEP_EX, unroll=4)
    def _(i):
        e = step * STEP_EX + i
        live = (ids_ref[pl.ds(e, 1), :] != 0).astype(jnp.bfloat16)
        g = jnp.dot(cots_ref[e] * live, acts_ref[i], preferred_element_type=jnp.float32)
        g = g * flip_ref[...]
        for low in range(2):
            tile = [g[:, (2 * q + low) * LANES:(2 * q + low + 1) * LANES] for q in range(tiles // 2)]
            tile = butterfly(tile)
            for q in range(tiles // 2):
                parts = butterfly([tile[q][8 * s:8 * s + 8] for s in range(rows // 8)])
                for s in range(rows // 8):
                    grad_ref[2 * q + low, pl.ds(e * stride + 8 * s, 8), :] = parts[s]

    @pl.when(step == pl.num_programs(0) - 1)
    def _():
        lane = lax.broadcasted_iota(jnp.int32, (TAP, LANES), 1)
        low_half = jnp.where(lane < LANES // 2, 1.0, -1.0).astype(jnp.float32)

        @pl.loop(0, (rows // 8) * (tiles // 2), unroll=4)
        def _(index):
            s = index // (tiles // 2)
            q = index % (tiles // 2)
            high, low = [], []
            for r in range(8):
                pieces = [
                    grad_ref.at[2 * q + j][pl.ds(s * 8 + r, n_ex, stride=stride), :] for j in range(2)
                ]
                x = jnp.concatenate(pieces, axis=1)
                h = x.astype(jnp.bfloat16)
                high.append(h)
                low.append((x - h.astype(jnp.float32)).astype(jnp.bfloat16))
            nt = (((1,), (1,)), ((), ()))
            mixed = lax.dot_general(walsh_ref[...], jnp.concatenate(high, axis=0), nt, preferred_element_type=jnp.float32)
            mixed += lax.dot_general(walsh_ref[...], jnp.concatenate(low, axis=0), nt, preferred_element_type=jnp.float32)
            parts = butterfly([mixed[:, j * LANES:(j + 1) * LANES] for j in range(4)])
            for j in range(4):
                v = parts[j]
                v = v * low_half + pltpu.roll(v, LANES // 2, 1)
                table_ref[pl.ds((s * 4 + j) * width + q * TAP, TAP), :] = v


def gather_kernel(segments, start, rows_ref, table_ref, half_ref, sign_ref, *refs):
    n_extra = sum(extra is not None for _, _, extra in segments)
    extras, out_ref, bufs = refs[:n_extra], refs[-3], refs[-2:]
    n_block = segments[-1][1]

    def fetch(block, slot):
        base = pl.multiple_of(block * LANES, LANES)
        for j in range(LANES):
            bufs[slot][j:j + 1, :] = table_ref[pl.ds(rows_ref[base + j], 1), :]

    def finish(block, t, extra, first):
        here = pl.ds(start + block, 1)
        picked = jnp.where(half_ref[here, :] > 0, t[LANES // 2:], t[:LANES // 2]) * sign_ref[here, :]
        out_ref[block] = picked if extra is None else picked + extras[extra][block - first]

    fetch(0, 0)
    for first, last, extra in segments:

        @pl.loop(first // 2, last // 2)
        def _(i):
            t = bufs[0][...].T
            fetch(2 * i + 1, 1)
            finish(2 * i, t, extra, first)
            t = bufs[1][...].T
            fetch(jnp.minimum(2 * i + 2, n_block - 1), 0)
            finish(2 * i + 1, t, extra, first)


def whole(shape):
    return pl.BlockSpec(shape, lambda i, *_: (0,) * len(shape))


def make_table(activations, cotangents, token_ids, signs):
    n_ex, toks, width = activations.shape
    slab = cotangents.shape[2]
    small = [
        pltpu.with_memory_space_constraint(x, pltpu.HBM)
        for x in (jnp.swapaxes(cotangents, 1, 2), token_ids, signs, jnp.asarray(walsh_table(TAP)))
    ]
    return pl.pallas_call(
        functools.partial(table_kernel, n_ex, width),
        out_shape=pltpu.VMEM((slab // 2 * width, LANES), jnp.float32),
        grid=(n_ex // STEP_EX,),
        in_specs=[
            pl.BlockSpec((STEP_EX, toks, width), lambda i: (i, 0, 0)),
        ] + [pl.BlockSpec(memory_space=pltpu.HBM)] * 4,
        out_specs=pl.BlockSpec(memory_space=pltpu.VMEM),
        scratch_shapes=[
            pltpu.VMEM((width // LANES, n_ex * (slab + EXTRA_ROWS), LANES), jnp.float32),
            pltpu.VMEM((slab, width), jnp.float32),
            pltpu.VMEM((n_ex, slab, toks), cotangents.dtype),
            pltpu.VMEM(token_ids.shape, token_ids.dtype),
            pltpu.VMEM(signs.shape, signs.dtype),
            pltpu.VMEM((TAP, TAP), jnp.bfloat16),
            pltpu.SemaphoreType.DMA((4,)),
        ],
        compiler_params=pltpu.CompilerParams(
            dimension_semantics=("arbitrary",), vmem_limit_bytes=26 * 1024 * 1024
        ),
        cost_estimate=pl.CostEstimate(flops=10**13, bytes_accessed=2**25, transcendentals=0),
        name="make_table",
    )(activations, *small)


def gather_rows(table, index, core, group, after=(), add=()):
    half, sign = index[:2]
    rows = index[2 + core * len(GROUPS) + group]
    n_block = rows.shape[0]
    start = (core * len(GROUPS) + group) * n_block
    segments, at = [], 0
    for number, (low, high, _) in enumerate(add):
        if at < low:
            segments.append((at, low, None))
        segments.append((low, high, number))
        at = high
    if at < n_block:
        segments.append((at, n_block, None))
    vmem = pl.BlockSpec(memory_space=pltpu.VMEM)
    n_add = len(add)

    def kernel(*refs):
        gather_kernel(segments, start, *refs[:4 + n_add], *refs[4 + n_add + len(after):])

    return pl.pallas_call(
        kernel,
        out_shape=jax.ShapeDtypeStruct((n_block, LANES // 2, LANES), jnp.float32),
        in_specs=[pl.BlockSpec(memory_space=pltpu.SMEM)] + [vmem] * (3 + n_add) + [pl.BlockSpec(memory_space=pl.ANY)] * len(after),
        out_specs=vmem,
        scratch_shapes=[pltpu.VMEM((LANES, LANES), jnp.float32)] * 2,
        compiler_params=pltpu.CompilerParams(vmem_limit_bytes=4 * 1024 * 1024),
        cost_estimate=pl.CostEstimate(
            flops=n_block * LANES * ROW_COST, bytes_accessed=n_block * LANES * 4096, transcendentals=0
        ),
        name="gather_rows",
    )(rows.reshape(-1), table, half, sign, *[x for _, _, x in add], *after)


GROUPS = (((2, 0), (2, 1)), ((1, 0), (3, 0)), ((1, 1), (3, 1)), ((0, 0), (0, 1)))
FAR, FIRST, SECOND, OWN = range(4)


def index_kernel(width, bits, me_ref, select_ref, half_ref, sign_ref, *rows_refs):
    me = me_ref[0]
    n_y, _, n_block, _ = select_ref.shape
    mid = n_block // 2
    col_bits, width_bits = D.bit_length() - 1, width.bit_length() - 1
    for core in range(2):
        owner_core = (me & 1) ^ (1 - core)
        for group, pieces in enumerate(GROUPS):
            for place, (step, part) in enumerate(pieces):
                chosen = select_ref[((me >> 1) + step) & (n_y - 1), owner_core, part * mid:(part + 1) * mid, :]
                row = chosen >> col_bits
                column = chosen & (D - 1)
                shared = (column >> width_bits) & me
                parity = jnp.zeros_like(shared)
                for bit in range(bits):
                    parity = parity ^ (shared >> bit & 1)
                here = pl.ds((core * len(GROUPS) + group) * n_block + place * mid, mid)
                rows = (row >> 1) * width + (column & (width - 1))
                rows_refs[core * len(GROUPS) + group][place * mid:(place + 1) * mid, :] = rows
                half_ref[here, :] = row & 1
                sign_ref[here, :] = (1 - 2 * parity).astype(jnp.float32)


def make_index(select, me, n_param, width):
    n_block = select.shape[0] // LANES
    vmem = pl.BlockSpec(memory_space=pltpu.VMEM)
    return pl.pallas_call(
        functools.partial(index_kernel, width, n_param.bit_length() - 1),
        out_shape=(
            jax.ShapeDtypeStruct((n_block, LANES), jnp.int32),
            jax.ShapeDtypeStruct((n_block, LANES), jnp.float32),
        ) + (jax.ShapeDtypeStruct((n_block // n_param, LANES), jnp.int32),) * n_param,
        in_specs=[pl.BlockSpec(memory_space=pltpu.SMEM), vmem],
        out_specs=(vmem,) * (2 + n_param),
        compiler_params=pltpu.CompilerParams(vmem_limit_bytes=4 * 1024 * 1024),
        name="make_index",
    )(me.reshape(1), select.reshape(n_param // 2, 2, n_block // n_param, LANES))


def gram_kernel(n_ex, core_ref, *refs):
    x_refs, out_ref, high_ref, low_ref, part_ref = refs[:-4], refs[-4], refs[-3], refs[-2], refs[-1]
    core = core_ref[0]
    blocks = x_refs[0].shape[0]
    half = LANES // 2
    for b in range(blocks):
        x = jnp.concatenate([r[b] for r in x_refs], axis=1)
        h = x.astype(jnp.bfloat16)
        low = (x - h.astype(jnp.float32)).astype(jnp.bfloat16)
        for at in ((b + 8, b - 8) if b >= 8 else (b + 8,)):
            high_ref[at * n_ex:(at + 1) * n_ex, :] = h
            low_ref[at * n_ex:(at + 1) * n_ex, :] = low
    left = lax.broadcasted_iota(jnp.int32, (n_ex // 2, LANES), 1) < half
    nt = (((1,), (1,)), ((), ()))

    @pl.loop(0, blocks // 4)
    def _(quad):
        rows = pl.ds(pl.multiple_of(quad * 4 * n_ex, 4 * n_ex), 12 * n_ex)
        columns = pl.ds(pl.multiple_of((quad * 4 + 8) * n_ex, 4 * n_ex), 4 * n_ex)
        t = lax.dot_general(high_ref[rows, :], high_ref[columns, :], nt, preferred_element_type=jnp.float32)
        t += lax.dot_general(high_ref[rows, :], low_ref[columns, :], nt, preferred_element_type=jnp.float32)
        t += lax.dot_general(low_ref[rows, :], high_ref[columns, :], nt, preferred_element_type=jnp.float32)
        part_ref[...] = t
        for v in range(4):
            lanes = slice(v // 2 * LANES, (v // 2 + 1) * LANES)
            for m in range(4):
                offset = 2 * m + core + 1
                first = pl.multiple_of((8 + v - offset) * n_ex, n_ex)
                top = part_ref[pl.ds(first, n_ex // 2), lanes]
                low = part_ref[pl.ds(first + n_ex // 2, n_ex // 2), lanes]
                strip = part_ref[pl.ds(pl.multiple_of((8 + v) * n_ex + 8 * (offset - 1), 8), 8), lanes]
                if v % 2:
                    top = pltpu.roll(top, half, 1)
                    strip = pltpu.roll(strip, half, 1)
                else:
                    low = pltpu.roll(low, half, 1)
                row_block = (quad * 4 + v + blocks - offset) & (blocks - 1)
                out_ref[m, row_block, :n_ex // 2, :] = jnp.where(left, top, low)
                out_ref[m, quad * 4 + v, n_ex // 2:, :] = strip


def partial_gram(shares, core):
    blocks, n_ex, _ = shares[0].shape
    width = len(shares) * LANES
    vmem = pl.BlockSpec(memory_space=pltpu.VMEM)
    return pl.pallas_call(
        functools.partial(gram_kernel, n_ex),
        out_shape=jax.ShapeDtypeStruct((4, blocks, n_ex // 2 + 8, LANES), jnp.float32),
        in_specs=[pl.BlockSpec(memory_space=pltpu.SMEM)] + [vmem] * len(shares),
        out_specs=vmem,
        scratch_shapes=[pltpu.VMEM(((blocks + 8) * n_ex, width), jnp.bfloat16)] * 2
        + [pltpu.VMEM((12 * n_ex, 4 * n_ex), jnp.float32)],
        compiler_params=pltpu.CompilerParams(vmem_limit_bytes=16 * 1024 * 1024),
        name="partial_gram",
    )(core.reshape(1), *shares)


def sum_kernel(scale, x_ref, tile_ref, strip_ref):
    half = LANES // 2
    total = jnp.sum(x_ref[...], axis=0) * scale
    pair = total[:half // 2]
    tile = jnp.concatenate([pair[:, :half], pair[:, half:]], axis=0)
    tile_ref[0] = tile
    tile_ref[1] = tile.T
    strip_ref[...] = total[half // 2:]


def sum_tiles(received):
    vmem = pl.BlockSpec(memory_space=pltpu.VMEM)
    return pl.pallas_call(
        functools.partial(sum_kernel, 1.0 / K),
        out_shape=(
            jax.ShapeDtypeStruct((2, LANES // 2, LANES // 2), jnp.float32),
            jax.ShapeDtypeStruct((8, LANES), jnp.float32),
        ),
        in_specs=[vmem],
        out_specs=(vmem, vmem),
        compiler_params=pltpu.CompilerParams(vmem_limit_bytes=4 * 1024 * 1024),
        name="sum_tiles",
    )(received)


def place_kernel(me_ref, x_ref, out_ref):
    half = LANES // 2
    count = out_ref.shape[1] // half
    columns = [None] * count
    columns[0] = jnp.concatenate([x_ref[p, half:, :half] for p in range(8)], axis=0)
    for p in range(8):
        columns[p + 1] = x_ref[p, :half, :half]
        if count - 1 - p > p + 1:
            columns[count - 1 - p] = x_ref[p, :half, half:]
    row = jnp.concatenate(columns, axis=1)
    out_ref[...] = pltpu.roll(row, me_ref[0] * half, 1)


def place_tiles(tiles, me, n_ex, count):
    vmem = pl.BlockSpec(memory_space=pltpu.VMEM)
    return pl.pallas_call(
        place_kernel,
        out_shape=jax.ShapeDtypeStruct((n_ex, count * n_ex), jnp.float32),
        in_specs=[pl.BlockSpec(memory_space=pltpu.SMEM), vmem],
        out_specs=vmem,
        compiler_params=pltpu.CompilerParams(vmem_limit_bytes=4 * 1024 * 1024),
        name="place_tiles",
    )(me.reshape(1), tiles)


def body(activations, cotangents, token_ids, signs, select):
    n_param, n_group = lax.axis_size("param"), lax.axis_size("ex")
    n_ex, _, width = activations.shape
    me = lax.axis_index("param")
    table = make_table(activations, cotangents, token_ids, signs)
    index = make_index(select, me, n_param, width)
    n_block = select.shape[0] // n_param // LANES
    n_y = n_param // 2
    swap = [(i, i ^ 1) for i in range(n_param)]

    def along(step):
        return [(i, (i + 2 * step) % n_param) for i in range(n_param)]

    mid = n_block // 2
    sent = gather_rows(table, index, 0, FAR)
    arrived = lax.ppermute(sent, "param", swap)
    far = gather_rows(table, index, 1, FAR, after=(sent,))
    outward = (far[:mid] + arrived[:mid], far[mid:] + arrived[mid:])
    up, down = lax.ppermute(outward[0], "param", along(1)), lax.ppermute(outward[1], "param", along(-1))
    sent_first = gather_rows(table, index, 0, FIRST, after=outward)
    arrived_first = lax.ppermute(sent_first, "param", swap)
    sent_second = gather_rows(table, index, 0, SECOND, after=(sent_first,))
    arrived_second = lax.ppermute(sent_second, "param", swap)
    sent = gather_rows(table, index, 0, OWN, after=(sent_second,))
    arrived = lax.ppermute(sent, "param", swap)
    first = gather_rows(table, index, 1, FIRST, after=(sent,), add=((0, mid, up),))
    outward = (first[:mid] + arrived_first[:mid], first[mid:] + arrived_first[mid:])
    first = lax.ppermute(outward[0], "param", along(1)), lax.ppermute(outward[1], "param", along(-1))
    second = gather_rows(table, index, 1, SECOND, after=outward, add=((mid, n_block, down),))
    outward = (second[:mid] + arrived_second[:mid], second[mid:] + arrived_second[mid:])
    second = lax.ppermute(outward[0], "param", along(1)), lax.ppermute(outward[1], "param", along(-1))
    own = gather_rows(table, index, 1, OWN, after=outward)
    front = own[:mid] + arrived[:mid] + first[0] + first[1]
    own, arrived, front = lax.optimization_barrier((own, arrived, front))
    back = own[mid:] + arrived[mid:] + second[0] + second[1]
    features = (front, back)
    shares = [lax.all_to_all(x, "ex", split_axis=0, concat_axis=0) for x in features]
    shares += [lax.ppermute(x, "param", swap) for x in shares]
    whole_features = jnp.swapaxes(jnp.concatenate(features, axis=0), 0, 1).reshape(n_ex, -1)

    partial = partial_gram(shares, me % 2)
    rows_out = partial.shape[2]
    everyone = ("param", "ex")
    alike = [
        [(2 * y + core) * n_group + e for y in range(n_y) for e in range(n_group)] for core in range(2)
    ]
    received = lax.all_to_all(
        partial.reshape(n_y * n_group, rows_out, LANES),
        everyone,
        split_axis=0,
        concat_axis=0,
        axis_index_groups=alike,
    )
    tile, strip = sum_tiles(received)
    onward = [
        (p * n_group + e, p * n_group + (e + p + 1) % n_group) for p in range(n_param) for e in range(n_group)
    ]
    turned = lax.ppermute(tile[1], everyone, onward)
    message = jnp.concatenate([jnp.concatenate([tile[0], turned], axis=1), strip], axis=0)
    spread = lax.all_to_all(
        jnp.broadcast_to(message[None], (n_param,) + message.shape), "param", split_axis=0, concat_axis=0
    )
    gram = place_tiles(spread, lax.axis_index("ex"), n_ex, n_group)
    return (whole_features, gram)


def solution(mesh):
    return jax.shard_map(
        body,
        mesh=mesh,
        in_specs=(
            P("ex", None, "param"),
            P("ex", None, None),
            P("ex", None),
            P(None, "param"),
            P(),
        ),
        out_specs=(P("ex", "param"), P("ex", None)),
        check_vma=False,
    )
```

```python
import functools
import math

import jax
import jax.numpy as jnp
import ml_dtypes
import numpy as np
from jax import lax
from jax.experimental import pallas as pl
from jax.experimental.pallas import tpu as pltpu
from jax.sharding import PartitionSpec as P

D = 8192
SLAB = 64
TOKS = 128
K = 32768
LANES = 128
ROW_COST = 10_000_000
STEP_EX = 8
TAP = 256
EXTRA_ROWS = 8


def walsh_table(order):
    table = np.ones((1, 1), np.float32)
    while table.shape[0] < order:
        table = np.block([[table, table], [table, -table]])
    return table.astype(ml_dtypes.bfloat16)


def butterfly(parts):
    count = len(parts)
    half = 1
    while half < count:
        out = list(parts)
        for index in range(count):
            if not index & half:
                out[index] = parts[index] + parts[index | half]
                out[index | half] = parts[index] - parts[index | half]
        parts = out
        half *= 2
    return parts


def table_kernel(n_ex, width, acts_ref, *refs):
    sources, (table_ref, grad_ref, flip_ref), copies, sems = refs[:4], refs[4:7], refs[7:11], refs[11]
    cots_ref, ids_ref, signs_ref, walsh_ref = copies
    step = pl.program_id(0)
    tiles = width // LANES
    rows = SLAB
    stride = SLAB + EXTRA_ROWS

    @pl.when(step == 0)
    def _():
        started = [pltpu.make_async_copy(a, b, sems.at[i]) for i, (a, b) in enumerate(zip(sources, copies))]
        for copy in started:
            copy.start()
        for copy in started:
            copy.wait()
        factor = 1.0 / math.sqrt(TOKS) / math.sqrt(SLAB * D)
        flip_ref[...] = signs_ref[...].astype(jnp.float32) * factor

    @pl.loop(0, STEP_EX, unroll=4)
    def _(i):
        e = step * STEP_EX + i
        live = (ids_ref[pl.ds(e, 1), :] != 0).astype(jnp.bfloat16)
        g = jnp.dot(cots_ref[e] * live, acts_ref[i], preferred_element_type=jnp.float32)
        g = g * flip_ref[...]
        for low in range(2):
            tile = [g[:, (2 * q + low) * LANES:(2 * q + low + 1) * LANES] for q in range(tiles // 2)]
            tile = butterfly(tile)
            for q in range(tiles // 2):
                parts = butterfly([tile[q][8 * s:8 * s + 8] for s in range(rows // 8)])
                for s in range(rows // 8):
                    grad_ref[2 * q + low, pl.ds(e * stride + 8 * s, 8), :] = parts[s]

    @pl.when(step == pl.num_programs(0) - 1)
    def _():
        lane = lax.broadcasted_iota(jnp.int32, (TAP, LANES), 1)
        low_half = jnp.where(lane < LANES // 2, 1.0, -1.0).astype(jnp.float32)

        @pl.loop(0, (rows // 8) * (tiles // 2), unroll=4)
        def _(index):
            s = index // (tiles // 2)
            q = index % (tiles // 2)
            high, low = [], []
            for r in range(8):
                pieces = [
                    grad_ref.at[2 * q + j][pl.ds(s * 8 + r, n_ex, stride=stride), :] for j in range(2)
                ]
                x = jnp.concatenate(pieces, axis=1)
                h = x.astype(jnp.bfloat16)
                high.append(h)
                low.append((x - h.astype(jnp.float32)).astype(jnp.bfloat16))
            nt = (((1,), (1,)), ((), ()))
            mixed = lax.dot_general(walsh_ref[...], jnp.concatenate(high, axis=0), nt, preferred_element_type=jnp.float32)
            mixed += lax.dot_general(walsh_ref[...], jnp.concatenate(low, axis=0), nt, preferred_element_type=jnp.float32)
            parts = butterfly([mixed[:, j * LANES:(j + 1) * LANES] for j in range(4)])
            for j in range(4):
                v = parts[j]
                v = v * low_half + pltpu.roll(v, LANES // 2, 1)
                table_ref[pl.ds((s * 4 + j) * width + q * TAP, TAP), :] = v


def gather_kernel(segments, start, rows_ref, table_ref, half_ref, sign_ref, *refs):
    n_extra = sum(extra is not None for _, _, extra in segments)
    extras, out_ref, bufs = refs[:n_extra], refs[-3], refs[-2:]
    n_block = segments[-1][1]

    def fetch(block, slot):
        base = pl.multiple_of(block * LANES, LANES)
        for j in range(LANES):
            bufs[slot][j:j + 1, :] = table_ref[pl.ds(rows_ref[base + j], 1), :]

    def finish(block, t, extra, first):
        here = pl.ds(start + block, 1)
        picked = jnp.where(half_ref[here, :] > 0, t[LANES // 2:], t[:LANES // 2]) * sign_ref[here, :]
        out_ref[block] = picked if extra is None else picked + extras[extra][block - first]

    fetch(0, 0)
    for first, last, extra in segments:

        @pl.loop(first // 2, last // 2)
        def _(i):
            t = bufs[0][...].T
            fetch(2 * i + 1, 1)
            finish(2 * i, t, extra, first)
            t = bufs[1][...].T
            fetch(jnp.minimum(2 * i + 2, n_block - 1), 0)
            finish(2 * i + 1, t, extra, first)


def whole(shape):
    return pl.BlockSpec(shape, lambda i, *_: (0,) * len(shape))


def make_table(activations, cotangents, token_ids, signs):
    n_ex, toks, width = activations.shape
    slab = cotangents.shape[2]
    small = [
        pltpu.with_memory_space_constraint(x, pltpu.HBM)
        for x in (jnp.swapaxes(cotangents, 1, 2), token_ids, signs, jnp.asarray(walsh_table(TAP)))
    ]
    return pl.pallas_call(
        functools.partial(table_kernel, n_ex, width),
        out_shape=pltpu.VMEM((slab // 2 * width, LANES), jnp.float32),
        grid=(n_ex // STEP_EX,),
        in_specs=[
            pl.BlockSpec((STEP_EX, toks, width), lambda i: (i, 0, 0)),
        ] + [pl.BlockSpec(memory_space=pltpu.HBM)] * 4,
        out_specs=pl.BlockSpec(memory_space=pltpu.VMEM),
        scratch_shapes=[
            pltpu.VMEM((width // LANES, n_ex * (slab + EXTRA_ROWS), LANES), jnp.float32),
            pltpu.VMEM((slab, width), jnp.float32),
            pltpu.VMEM((n_ex, slab, toks), cotangents.dtype),
            pltpu.VMEM(token_ids.shape, token_ids.dtype),
            pltpu.VMEM(signs.shape, signs.dtype),
            pltpu.VMEM((TAP, TAP), jnp.bfloat16),
            pltpu.SemaphoreType.DMA((4,)),
        ],
        compiler_params=pltpu.CompilerParams(
            dimension_semantics=("arbitrary",), vmem_limit_bytes=26 * 1024 * 1024
        ),
        cost_estimate=pl.CostEstimate(flops=10**13, bytes_accessed=2**25, transcendentals=0),
        name="make_table",
    )(activations, *small)


def gather_rows(table, index, core, group, after=(), add=()):
    half, sign = index[:2]
    rows = index[2 + core * len(GROUPS) + group]
    n_block = rows.shape[0]
    start = (core * len(GROUPS) + group) * n_block
    segments, at = [], 0
    for number, (low, high, _) in enumerate(add):
        if at < low:
            segments.append((at, low, None))
        segments.append((low, high, number))
        at = high
    if at < n_block:
        segments.append((at, n_block, None))
    vmem = pl.BlockSpec(memory_space=pltpu.VMEM)
    n_add = len(add)

    def kernel(*refs):
        gather_kernel(segments, start, *refs[:4 + n_add], *refs[4 + n_add + len(after):])

    return pl.pallas_call(
        kernel,
        out_shape=jax.ShapeDtypeStruct((n_block, LANES // 2, LANES), jnp.float32),
        in_specs=[pl.BlockSpec(memory_space=pltpu.SMEM)] + [vmem] * (3 + n_add) + [pl.BlockSpec(memory_space=pl.ANY)] * len(after),
        out_specs=vmem,
        scratch_shapes=[pltpu.VMEM((LANES, LANES), jnp.float32)] * 2,
        compiler_params=pltpu.CompilerParams(vmem_limit_bytes=4 * 1024 * 1024),
        cost_estimate=pl.CostEstimate(
            flops=n_block * LANES * ROW_COST, bytes_accessed=n_block * LANES * 4096, transcendentals=0
        ),
        name="gather_rows",
    )(rows.reshape(-1), table, half, sign, *[x for _, _, x in add], *after)


GROUPS = (((2, 0), (2, 1)), ((1, 0), (3, 0)), ((1, 1), (3, 1)), ((0, 0), (0, 1)))
FAR, FIRST, SECOND, OWN = range(4)


def index_kernel(width, bits, me_ref, select_ref, table_ref, half_ref, sign_ref, *rows_refs):
    me = me_ref[0]
    n_y, _, n_block, _ = select_ref.shape
    mid = n_block // 2
    col_bits, width_bits = D.bit_length() - 1, width.bit_length() - 1
    for core in range(2):
        owner_core = (me & 1) ^ (1 - core)
        for group, pieces in enumerate(GROUPS):
            for place, (step, part) in enumerate(pieces):
                chosen = select_ref[((me >> 1) + step) & (n_y - 1), owner_core, part * mid:(part + 1) * mid, :]
                row = chosen >> col_bits
                column = chosen & (D - 1)
                shared = (column >> width_bits) & me
                parity = jnp.zeros_like(shared)
                for bit in range(bits):
                    parity = parity ^ (shared >> bit & 1)
                here = pl.ds((core * len(GROUPS) + group) * n_block + place * mid, mid)
                rows = (row >> 1) * width + (column & (width - 1))
                rows_refs[core * len(GROUPS) + group][place * mid:(place + 1) * mid, :] = rows
                half_ref[here, :] = row & 1
                sign_ref[here, :] = (1 - 2 * parity).astype(jnp.float32)


def make_index(select, me, n_param, width, after):
    n_block = select.shape[0] // LANES
    vmem = pl.BlockSpec(memory_space=pltpu.VMEM)
    return pl.pallas_call(
        functools.partial(index_kernel, width, n_param.bit_length() - 1),
        out_shape=(
            jax.ShapeDtypeStruct((n_block, LANES), jnp.int32),
            jax.ShapeDtypeStruct((n_block, LANES), jnp.float32),
        ) + (jax.ShapeDtypeStruct((n_block // n_param, LANES), jnp.int32),) * n_param,
        in_specs=[pl.BlockSpec(memory_space=pltpu.SMEM), vmem, pl.BlockSpec(memory_space=pl.ANY)],
        out_specs=(vmem,) * (2 + n_param),
        compiler_params=pltpu.CompilerParams(vmem_limit_bytes=4 * 1024 * 1024),
        name="make_index",
    )(me.reshape(1), select.reshape(n_param // 2, 2, n_block // n_param, LANES), after)


def gram_kernel(n_ex, core_ref, *refs):
    x_refs, out_ref, high_ref, low_ref, part_ref = refs[:-4], refs[-4], refs[-3], refs[-2], refs[-1]
    core = core_ref[0]
    blocks = x_refs[0].shape[0]
    half = LANES // 2
    for b in range(blocks):
        x = jnp.concatenate([r[b] for r in x_refs], axis=1)
        h = x.astype(jnp.bfloat16)
        low = (x - h.astype(jnp.float32)).astype(jnp.bfloat16)
        for at in ((b + 8, b - 8) if b >= 8 else (b + 8,)):
            high_ref[at * n_ex:(at + 1) * n_ex, :] = h
            low_ref[at * n_ex:(at + 1) * n_ex, :] = low
    left = lax.broadcasted_iota(jnp.int32, (n_ex // 2, LANES), 1) < half
    nt = (((1,), (1,)), ((), ()))

    @pl.loop(0, blocks // 4)
    def _(quad):
        rows = pl.ds(pl.multiple_of(quad * 4 * n_ex, 4 * n_ex), 12 * n_ex)
        columns = pl.ds(pl.multiple_of((quad * 4 + 8) * n_ex, 4 * n_ex), 4 * n_ex)
        t = lax.dot_general(high_ref[rows, :], high_ref[columns, :], nt, preferred_element_type=jnp.float32)
        t += lax.dot_general(high_ref[rows, :], low_ref[columns, :], nt, preferred_element_type=jnp.float32)
        t += lax.dot_general(low_ref[rows, :], high_ref[columns, :], nt, preferred_element_type=jnp.float32)
        part_ref[...] = t
        for v in range(4):
            lanes = slice(v // 2 * LANES, (v // 2 + 1) * LANES)
            for m in range(4):
                offset = 2 * m + core + 1
                first = pl.multiple_of((8 + v - offset) * n_ex, n_ex)
                top = part_ref[pl.ds(first, n_ex // 2), lanes]
                low = part_ref[pl.ds(first + n_ex // 2, n_ex // 2), lanes]
                if v % 2:
                    top = pltpu.roll(top, half, 1)
                else:
                    low = pltpu.roll(low, half, 1)
                row_block = (quad * 4 + v + blocks - offset) & (blocks - 1)
                out_ref[m, row_block] = jnp.where(left, top, low)


def partial_gram(shares, core):
    blocks, n_ex, _ = shares[0].shape
    width = len(shares) * LANES
    vmem = pl.BlockSpec(memory_space=pltpu.VMEM)
    return pl.pallas_call(
        functools.partial(gram_kernel, n_ex),
        out_shape=jax.ShapeDtypeStruct((4, blocks, n_ex // 2, LANES), jnp.float32),
        in_specs=[pl.BlockSpec(memory_space=pltpu.SMEM)] + [vmem] * len(shares),
        out_specs=vmem,
        scratch_shapes=[pltpu.VMEM(((blocks + 8) * n_ex, width), jnp.bfloat16)] * 2
        + [pltpu.VMEM((12 * n_ex, 4 * n_ex), jnp.float32)],
        compiler_params=pltpu.CompilerParams(vmem_limit_bytes=16 * 1024 * 1024),
        name="partial_gram",
    )(core.reshape(1), *shares)


def halves_side_by_side(tile):
    rows = tile.shape[0] // 2
    return jnp.concatenate([tile[:rows], tile[rows:]], axis=1)


def halves_stacked(pair):
    lanes = pair.shape[1] // 2
    return jnp.concatenate([pair[:, :lanes], pair[:, lanes:]], axis=0)


def diagonal_kernel(*refs):
    out_ref = refs[-1]
    nt = (((1,), (1,)), ((), ()))
    same = cross = 0.0
    for ref in refs[:-1]:
        x = jnp.concatenate([ref[b] for b in range(ref.shape[0])], axis=1)
        high = x.astype(jnp.bfloat16)
        low = (x - high.astype(jnp.float32)).astype(jnp.bfloat16)
        same += lax.dot_general(high, high, nt, preferred_element_type=jnp.float32)
        cross += lax.dot_general(high, low, nt, preferred_element_type=jnp.float32)
    out_ref[...] = halves_side_by_side((same + cross + cross.T) * (1.0 / K))


def diagonal_part(features):
    n_ex = features[0].shape[1]
    vmem = pl.BlockSpec(memory_space=pltpu.VMEM)
    return pl.pallas_call(
        diagonal_kernel,
        out_shape=jax.ShapeDtypeStruct((n_ex // 2, 2 * n_ex), jnp.float32),
        in_specs=[vmem] * len(features),
        out_specs=vmem,
        compiler_params=pltpu.CompilerParams(vmem_limit_bytes=8 * 1024 * 1024),
        cost_estimate=pl.CostEstimate(flops=4 * 10**9, bytes_accessed=2**20, transcendentals=0),
        name="diagonal_part",
    )(*features)


def sum_kernel(x_ref, tile_ref, turned_ref):
    tile = halves_stacked(jnp.sum(x_ref[...], axis=0) * (1.0 / K))
    tile_ref[...] = tile
    turned_ref[...] = tile.T


def sum_tiles(received):
    n_ex = 2 * received.shape[1]
    vmem = pl.BlockSpec(memory_space=pltpu.VMEM)
    return pl.pallas_call(
        sum_kernel,
        out_shape=(jax.ShapeDtypeStruct((n_ex, n_ex), jnp.float32),) * 2,
        in_specs=[vmem],
        out_specs=(vmem, vmem),
        compiler_params=pltpu.CompilerParams(vmem_limit_bytes=4 * 1024 * 1024),
        name="sum_tiles",
    )(received)


def message_kernel(tile_ref, turned_ref, part_ref, out_ref):
    n_ex = tile_ref.shape[0]
    pair = jnp.concatenate([tile_ref[...], turned_ref[...]], axis=1)
    for p in range(out_ref.shape[0]):
        out_ref[p, :n_ex, :] = pair
        out_ref[p, n_ex:, :] = part_ref[...]


def messages(tile, turned, part, count):
    rows = tile.shape[0] + part.shape[0]
    vmem = pl.BlockSpec(memory_space=pltpu.VMEM)
    return pl.pallas_call(
        message_kernel,
        out_shape=jax.ShapeDtypeStruct((count, rows, LANES), jnp.float32),
        in_specs=[vmem] * 3,
        out_specs=vmem,
        compiler_params=pltpu.CompilerParams(vmem_limit_bytes=4 * 1024 * 1024),
        name="messages",
    )(tile, turned, part)


def place_kernel(me_ref, x_ref, out_ref):
    half = LANES // 2
    count = out_ref.shape[1] // half
    columns = [None] * count
    columns[0] = halves_stacked(jnp.sum(x_ref[:, half:, :], axis=0))
    for p in range(8):
        columns[p + 1] = x_ref[p, :half, :half]
        if count - 1 - p > p + 1:
            columns[count - 1 - p] = x_ref[p, :half, half:]
    row = jnp.concatenate(columns, axis=1)
    out_ref[...] = pltpu.roll(row, me_ref[0] * half, 1)


def place_tiles(tiles, me, n_ex, count):
    vmem = pl.BlockSpec(memory_space=pltpu.VMEM)
    return pl.pallas_call(
        place_kernel,
        out_shape=jax.ShapeDtypeStruct((n_ex, count * n_ex), jnp.float32),
        in_specs=[pl.BlockSpec(memory_space=pltpu.SMEM), vmem],
        out_specs=vmem,
        compiler_params=pltpu.CompilerParams(vmem_limit_bytes=4 * 1024 * 1024),
        name="place_tiles",
    )(me.reshape(1), tiles)


def body(activations, cotangents, token_ids, signs, select):
    n_param, n_group = lax.axis_size("param"), lax.axis_size("ex")
    n_ex, _, width = activations.shape
    me = lax.axis_index("param")
    table = make_table(activations, cotangents, token_ids, signs)
    index = make_index(select, me, n_param, width, table)
    n_block = select.shape[0] // n_param // LANES
    n_y = n_param // 2
    swap = [(i, i ^ 1) for i in range(n_param)]

    def along(step):
        return [(i, (i + 2 * step) % n_param) for i in range(n_param)]

    mid = n_block // 2
    sent = gather_rows(table, index, 0, FAR)
    arrived = lax.ppermute(sent, "param", swap)
    far = gather_rows(table, index, 1, FAR, after=(sent,))
    outward = (far[:mid] + arrived[:mid], far[mid:] + arrived[mid:])
    up, down = lax.ppermute(outward[0], "param", along(1)), lax.ppermute(outward[1], "param", along(-1))
    sent_first = gather_rows(table, index, 0, FIRST, after=outward)
    arrived_first = lax.ppermute(sent_first, "param", swap)
    sent_second = gather_rows(table, index, 0, SECOND, after=(sent_first,))
    arrived_second = lax.ppermute(sent_second, "param", swap)
    sent = gather_rows(table, index, 0, OWN, after=(sent_second,))
    arrived = lax.ppermute(sent, "param", swap)
    first = gather_rows(table, index, 1, FIRST, after=(sent,), add=((0, mid, up),))
    outward = (first[:mid] + arrived_first[:mid], first[mid:] + arrived_first[mid:])
    first = lax.ppermute(outward[0], "param", along(1)), lax.ppermute(outward[1], "param", along(-1))
    second = gather_rows(table, index, 1, SECOND, after=outward, add=((mid, n_block, down),))
    outward = (second[:mid] + arrived_second[:mid], second[mid:] + arrived_second[mid:])
    second = lax.ppermute(outward[0], "param", along(1)), lax.ppermute(outward[1], "param", along(-1))
    own = gather_rows(table, index, 1, OWN, after=outward)
    front = own[:mid] + arrived[:mid] + first[0] + first[1]
    own, arrived, front = lax.optimization_barrier((own, arrived, front))
    back = own[mid:] + arrived[mid:] + second[0] + second[1]
    features = (front, back)
    shares = [lax.all_to_all(x, "ex", split_axis=0, concat_axis=0) for x in features]
    shares += [lax.ppermute(x, "param", swap) for x in shares]
    whole_features = jnp.swapaxes(jnp.concatenate(features, axis=0), 0, 1).reshape(n_ex, -1)

    partial = partial_gram(shares, me % 2)
    rows_out = partial.shape[2]
    everyone = ("param", "ex")
    alike = [
        [(2 * y + core) * n_group + e for y in range(n_y) for e in range(n_group)] for core in range(2)
    ]
    received = lax.all_to_all(
        partial.reshape(n_y * n_group, rows_out, LANES),
        everyone,
        split_axis=0,
        concat_axis=0,
        axis_index_groups=alike,
    )
    tile, turned = sum_tiles(received)
    onward = [
        (p * n_group + e, p * n_group + (e + p + 1) % n_group) for p in range(n_param) for e in range(n_group)
    ]
    turned = lax.ppermute(turned, everyone, onward)
    spread = lax.all_to_all(
        messages(tile, turned, diagonal_part(features), n_param), "param", split_axis=0, concat_axis=0
    )
    gram = place_tiles(spread, lax.axis_index("ex"), n_ex, n_group)
    return (whole_features, gram)


def solution(mesh):
    return jax.shard_map(
        body,
        mesh=mesh,
        in_specs=(
            P("ex", None, "param"),
            P("ex", None, None),
            P("ex", None),
            P(None, "param"),
            P(),
        ),
        out_specs=(P("ex", "param"), P("ex", None)),
        check_vma=False,
    )
```

```python
import functools
import math

import jax
import jax.numpy as jnp
import ml_dtypes
import numpy as np
from jax import lax
from jax.experimental import pallas as pl
from jax.experimental.pallas import tpu as pltpu
from jax.sharding import PartitionSpec as P

D = 8192
SLAB = 64
TOKS = 128
K = 32768
LANES = 128
ROW_COST = 10_000_000
STEP_EX = 8
TAP = 256
EXTRA_ROWS = 8


def walsh_table(order):
    table = np.ones((1, 1), np.float32)
    while table.shape[0] < order:
        table = np.block([[table, table], [table, -table]])
    return table.astype(ml_dtypes.bfloat16)


def butterfly(parts):
    count = len(parts)
    half = 1
    while half < count:
        out = list(parts)
        for index in range(count):
            if not index & half:
                out[index] = parts[index] + parts[index | half]
                out[index | half] = parts[index] - parts[index | half]
        parts = out
        half *= 2
    return parts


def table_kernel(n_ex, width, acts_ref, *refs):
    sources, (table_ref, grad_ref, flip_ref), copies, sems = refs[:4], refs[4:7], refs[7:11], refs[11]
    cots_ref, ids_ref, signs_ref, walsh_ref = copies
    step = pl.program_id(0)
    tiles = width // LANES
    rows = SLAB
    stride = SLAB + EXTRA_ROWS

    @pl.when(step == 0)
    def _():
        started = [pltpu.make_async_copy(a, b, sems.at[i]) for i, (a, b) in enumerate(zip(sources, copies))]
        for copy in started:
            copy.start()
        for copy in started:
            copy.wait()
        factor = 1.0 / math.sqrt(TOKS) / math.sqrt(SLAB * D)
        flip_ref[...] = signs_ref[...].astype(jnp.float32) * factor

    @pl.loop(0, STEP_EX, unroll=4)
    def _(i):
        e = step * STEP_EX + i
        live = (ids_ref[pl.ds(e, 1), :] != 0).astype(jnp.bfloat16)
        g = jnp.dot(cots_ref[e] * live, acts_ref[i], preferred_element_type=jnp.float32)
        g = g * flip_ref[...]
        for low in range(2):
            tile = [g[:, (2 * q + low) * LANES:(2 * q + low + 1) * LANES] for q in range(tiles // 2)]
            tile = butterfly(tile)
            for q in range(tiles // 2):
                parts = butterfly([tile[q][8 * s:8 * s + 8] for s in range(rows // 8)])
                for s in range(rows // 8):
                    grad_ref[2 * q + low, pl.ds(e * stride + 8 * s, 8), :] = parts[s]

    @pl.when(step == pl.num_programs(0) - 1)
    def _():
        lane = lax.broadcasted_iota(jnp.int32, (TAP, LANES), 1)
        low_half = jnp.where(lane < LANES // 2, 1.0, -1.0).astype(jnp.float32)

        @pl.loop(0, (rows // 8) * (tiles // 2), unroll=4)
        def _(index):
            s = index // (tiles // 2)
            q = index % (tiles // 2)
            high, low = [], []
            for r in range(8):
                pieces = [
                    grad_ref.at[2 * q + j][pl.ds(s * 8 + r, n_ex, stride=stride), :] for j in range(2)
                ]
                x = jnp.concatenate(pieces, axis=1)
                h = x.astype(jnp.bfloat16)
                high.append(h)
                low.append((x - h.astype(jnp.float32)).astype(jnp.bfloat16))
            nt = (((1,), (1,)), ((), ()))
            mixed = lax.dot_general(walsh_ref[...], jnp.concatenate(high, axis=0), nt, preferred_element_type=jnp.float32)
            mixed += lax.dot_general(walsh_ref[...], jnp.concatenate(low, axis=0), nt, preferred_element_type=jnp.float32)
            parts = butterfly([mixed[:, j * LANES:(j + 1) * LANES] for j in range(4)])
            for j in range(4):
                v = parts[j]
                v = v * low_half + pltpu.roll(v, LANES // 2, 1)
                table_ref[pl.ds((s * 4 + j) * width + q * TAP, TAP), :] = v


def gather_kernel(start, rows_ref, table_ref, half_ref, sign_ref, *refs):
    out_ref, bufs = refs[-3], refs[-2:]
    n_block = out_ref.shape[0]

    def fetch(block, slot):
        base = pl.multiple_of(block * LANES, LANES)
        for j in range(LANES):
            bufs[slot][j:j + 1, :] = table_ref[pl.ds(rows_ref[base + j], 1), :]

    def finish(block, t):
        here = pl.ds(start + block, 1)
        picked = jnp.where(half_ref[here, :] > 0, t[LANES // 2:], t[:LANES // 2])
        out_ref[block] = picked * sign_ref[here, :]

    fetch(0, 0)

    @pl.loop(0, n_block // 2)
    def _(i):
        t = bufs[0][...].T
        fetch(2 * i + 1, 1)
        finish(2 * i, t)
        t = bufs[1][...].T
        fetch(jnp.minimum(2 * i + 2, n_block - 1), 0)
        finish(2 * i + 1, t)


def whole(shape):
    return pl.BlockSpec(shape, lambda i, *_: (0,) * len(shape))


def make_table(activations, cotangents, token_ids, signs):
    n_ex, toks, width = activations.shape
    slab = cotangents.shape[2]
    small = [
        pltpu.with_memory_space_constraint(x, pltpu.HBM)
        for x in (jnp.swapaxes(cotangents, 1, 2), token_ids, signs, jnp.asarray(walsh_table(TAP)))
    ]
    return pl.pallas_call(
        functools.partial(table_kernel, n_ex, width),
        out_shape=pltpu.VMEM((slab // 2 * width, LANES), jnp.float32),
        grid=(n_ex // STEP_EX,),
        in_specs=[
            pl.BlockSpec((STEP_EX, toks, width), lambda i: (i, 0, 0)),
        ] + [pl.BlockSpec(memory_space=pltpu.HBM)] * 4,
        out_specs=pl.BlockSpec(memory_space=pltpu.VMEM),
        scratch_shapes=[
            pltpu.VMEM((width // LANES, n_ex * (slab + EXTRA_ROWS), LANES), jnp.float32),
            pltpu.VMEM((slab, width), jnp.float32),
            pltpu.VMEM((n_ex, slab, toks), cotangents.dtype),
            pltpu.VMEM(token_ids.shape, token_ids.dtype),
            pltpu.VMEM(signs.shape, signs.dtype),
            pltpu.VMEM((TAP, TAP), jnp.bfloat16),
            pltpu.SemaphoreType.DMA((4,)),
        ],
        compiler_params=pltpu.CompilerParams(
            dimension_semantics=("arbitrary",), vmem_limit_bytes=26 * 1024 * 1024
        ),
        cost_estimate=pl.CostEstimate(flops=10**13, bytes_accessed=2**25, transcendentals=0),
        name="make_table",
    )(activations, *small)


def gather_rows(table, index, core, group, after=()):
    half, sign = index[:2]
    rows = index[2 + core * len(GROUPS) + group]
    n_block = rows.shape[0]
    start = (core * len(GROUPS) + group) * n_block
    vmem = pl.BlockSpec(memory_space=pltpu.VMEM)
    return pl.pallas_call(
        functools.partial(gather_kernel, start),
        out_shape=jax.ShapeDtypeStruct((n_block, LANES // 2, LANES), jnp.float32),
        in_specs=[pl.BlockSpec(memory_space=pltpu.SMEM)] + [vmem] * 3
        + [pl.BlockSpec(memory_space=pl.ANY)] * len(after),
        out_specs=vmem,
        scratch_shapes=[pltpu.VMEM((LANES, LANES), jnp.float32)] * 2,
        compiler_params=pltpu.CompilerParams(vmem_limit_bytes=4 * 1024 * 1024),
        cost_estimate=pl.CostEstimate(
            flops=n_block * LANES * ROW_COST, bytes_accessed=n_block * LANES * 4096, transcendentals=0
        ),
        name="gather_rows",
    )(rows.reshape(-1), table, half, sign, *after)


GROUPS = (((2, 0), (2, 1)), ((1, 0), (3, 0)), ((1, 1), (3, 1)), ((0, 0), (0, 1)))
FAR, FIRST, SECOND, OWN = range(4)


def index_kernel(width, bits, me_ref, select_ref, table_ref, half_ref, sign_ref, *rows_refs):
    me = me_ref[0]
    n_y, _, n_block, _ = select_ref.shape
    mid = n_block // 2
    col_bits, width_bits = D.bit_length() - 1, width.bit_length() - 1
    for core in range(2):
        owner_core = (me & 1) ^ (1 - core)
        for group, pieces in enumerate(GROUPS):
            for place, (step, part) in enumerate(pieces):
                chosen = select_ref[((me >> 1) + step) & (n_y - 1), owner_core, part * mid:(part + 1) * mid, :]
                row = chosen >> col_bits
                column = chosen & (D - 1)
                shared = (column >> width_bits) & me
                parity = jnp.zeros_like(shared)
                for bit in range(bits):
                    parity = parity ^ (shared >> bit & 1)
                here = pl.ds((core * len(GROUPS) + group) * n_block + place * mid, mid)
                rows = (row >> 1) * width + (column & (width - 1))
                rows_refs[core * len(GROUPS) + group][place * mid:(place + 1) * mid, :] = rows
                half_ref[here, :] = row & 1
                sign_ref[here, :] = (1 - 2 * parity).astype(jnp.float32)


def make_index(select, me, n_param, width, after):
    n_block = select.shape[0] // LANES
    vmem = pl.BlockSpec(memory_space=pltpu.VMEM)
    return pl.pallas_call(
        functools.partial(index_kernel, width, n_param.bit_length() - 1),
        out_shape=(
            jax.ShapeDtypeStruct((n_block, LANES), jnp.int32),
            jax.ShapeDtypeStruct((n_block, LANES), jnp.float32),
        ) + (jax.ShapeDtypeStruct((n_block // n_param, LANES), jnp.int32),) * n_param,
        in_specs=[pl.BlockSpec(memory_space=pltpu.SMEM), vmem, pl.BlockSpec(memory_space=pl.ANY)],
        out_specs=(vmem,) * (2 + n_param),
        compiler_params=pltpu.CompilerParams(vmem_limit_bytes=4 * 1024 * 1024),
        name="make_index",
    )(me.reshape(1), select.reshape(n_param // 2, 2, n_block // n_param, LANES), after)


def gram_kernel(n_ex, core_ref, *refs):
    x_refs, out_ref, high_ref, low_ref, part_ref = refs[:-4], refs[-4], refs[-3], refs[-2], refs[-1]
    core = core_ref[0]
    blocks = x_refs[0].shape[0]
    half = LANES // 2
    for b in range(blocks):
        x = jnp.concatenate([r[b] for r in x_refs], axis=1)
        h = x.astype(jnp.bfloat16)
        low = (x - h.astype(jnp.float32)).astype(jnp.bfloat16)
        for at in ((b + 8, b - 8) if b >= 8 else (b + 8,)):
            high_ref[at * n_ex:(at + 1) * n_ex, :] = h
            low_ref[at * n_ex:(at + 1) * n_ex, :] = low
    left = lax.broadcasted_iota(jnp.int32, (n_ex // 2, LANES), 1) < half
    nt = (((1,), (1,)), ((), ()))

    @pl.loop(0, blocks // 4)
    def _(quad):
        rows = pl.ds(pl.multiple_of(quad * 4 * n_ex, 4 * n_ex), 12 * n_ex)
        columns = pl.ds(pl.multiple_of((quad * 4 + 8) * n_ex, 4 * n_ex), 4 * n_ex)
        t = lax.dot_general(high_ref[rows, :], high_ref[columns, :], nt, preferred_element_type=jnp.float32)
        t += lax.dot_general(high_ref[rows, :], low_ref[columns, :], nt, preferred_element_type=jnp.float32)
        t += lax.dot_general(low_ref[rows, :], high_ref[columns, :], nt, preferred_element_type=jnp.float32)
        part_ref[...] = t
        for v in range(4):
            lanes = slice(v // 2 * LANES, (v // 2 + 1) * LANES)
            for m in range(4):
                offset = 2 * m + core + 1
                first = pl.multiple_of((8 + v - offset) * n_ex, n_ex)
                top = part_ref[pl.ds(first, n_ex // 2), lanes]
                low = part_ref[pl.ds(first + n_ex // 2, n_ex // 2), lanes]
                if v % 2:
                    top = pltpu.roll(top, half, 1)
                else:
                    low = pltpu.roll(low, half, 1)
                row_block = (quad * 4 + v + blocks - offset) & (blocks - 1)
                out_ref[m, row_block] = jnp.where(left, top, low)


def partial_gram(shares, core):
    blocks, n_ex, _ = shares[0].shape
    width = len(shares) * LANES
    vmem = pl.BlockSpec(memory_space=pltpu.VMEM)
    return pl.pallas_call(
        functools.partial(gram_kernel, n_ex),
        out_shape=jax.ShapeDtypeStruct((4, blocks, n_ex // 2, LANES), jnp.float32),
        in_specs=[pl.BlockSpec(memory_space=pltpu.SMEM)] + [vmem] * len(shares),
        out_specs=vmem,
        scratch_shapes=[pltpu.VMEM(((blocks + 8) * n_ex, width), jnp.bfloat16)] * 2
        + [pltpu.VMEM((12 * n_ex, 4 * n_ex), jnp.float32)],
        compiler_params=pltpu.CompilerParams(vmem_limit_bytes=16 * 1024 * 1024),
        name="partial_gram",
    )(core.reshape(1), *shares)


def halves_side_by_side(tile):
    rows = tile.shape[0] // 2
    return jnp.concatenate([tile[:rows], tile[rows:]], axis=1)


def halves_stacked(pair):
    lanes = pair.shape[1] // 2
    return jnp.concatenate([pair[:, :lanes], pair[:, lanes:]], axis=0)


def diagonal_kernel(*refs):
    out_ref = refs[-1]
    nt = (((1,), (1,)), ((), ()))
    same = cross = 0.0
    for ref in refs[:-1]:
        x = jnp.concatenate([ref[b] for b in range(ref.shape[0])], axis=1)
        high = x.astype(jnp.bfloat16)
        low = (x - high.astype(jnp.float32)).astype(jnp.bfloat16)
        same += lax.dot_general(high, high, nt, preferred_element_type=jnp.float32)
        cross += lax.dot_general(high, low, nt, preferred_element_type=jnp.float32)
    out_ref[...] = halves_side_by_side((same + cross + cross.T) * (1.0 / K))


def diagonal_part(features):
    n_ex = features[0].shape[1]
    vmem = pl.BlockSpec(memory_space=pltpu.VMEM)
    return pl.pallas_call(
        diagonal_kernel,
        out_shape=jax.ShapeDtypeStruct((n_ex // 2, 2 * n_ex), jnp.float32),
        in_specs=[vmem] * len(features),
        out_specs=vmem,
        compiler_params=pltpu.CompilerParams(vmem_limit_bytes=8 * 1024 * 1024),
        cost_estimate=pl.CostEstimate(flops=4 * 10**9, bytes_accessed=2**20, transcendentals=0),
        name="diagonal_part",
    )(*features)


def sum_kernel(x_ref, tile_ref, turned_ref):
    tile = halves_stacked(jnp.sum(x_ref[...], axis=0) * (1.0 / K))
    tile_ref[...] = tile
    turned_ref[...] = tile.T


def sum_tiles(received):
    n_ex = 2 * received.shape[1]
    vmem = pl.BlockSpec(memory_space=pltpu.VMEM)
    return pl.pallas_call(
        sum_kernel,
        out_shape=(jax.ShapeDtypeStruct((n_ex, n_ex), jnp.float32),) * 2,
        in_specs=[vmem],
        out_specs=(vmem, vmem),
        compiler_params=pltpu.CompilerParams(vmem_limit_bytes=4 * 1024 * 1024),
        name="sum_tiles",
    )(received)


def message_kernel(tile_ref, turned_ref, part_ref, out_ref):
    n_ex = tile_ref.shape[0]
    pair = jnp.concatenate([tile_ref[...], turned_ref[...]], axis=1)
    for p in range(out_ref.shape[0]):
        out_ref[p, :n_ex, :] = pair
        out_ref[p, n_ex:, :] = part_ref[...]


def messages(tile, turned, part, count):
    rows = tile.shape[0] + part.shape[0]
    vmem = pl.BlockSpec(memory_space=pltpu.VMEM)
    return pl.pallas_call(
        message_kernel,
        out_shape=jax.ShapeDtypeStruct((count, rows, LANES), jnp.float32),
        in_specs=[vmem] * 3,
        out_specs=vmem,
        compiler_params=pltpu.CompilerParams(vmem_limit_bytes=4 * 1024 * 1024),
        name="messages",
    )(tile, turned, part)


def place_kernel(me_ref, x_ref, out_ref):
    half = LANES // 2
    count = out_ref.shape[1] // half
    columns = [None] * count
    columns[0] = halves_stacked(jnp.sum(x_ref[:, half:, :], axis=0))
    for p in range(8):
        columns[p + 1] = x_ref[p, :half, :half]
        if count - 1 - p > p + 1:
            columns[count - 1 - p] = x_ref[p, :half, half:]
    row = jnp.concatenate(columns, axis=1)
    out_ref[...] = pltpu.roll(row, me_ref[0] * half, 1)


def place_tiles(tiles, me, n_ex, count):
    vmem = pl.BlockSpec(memory_space=pltpu.VMEM)
    return pl.pallas_call(
        place_kernel,
        out_shape=jax.ShapeDtypeStruct((n_ex, count * n_ex), jnp.float32),
        in_specs=[pl.BlockSpec(memory_space=pltpu.SMEM), vmem],
        out_specs=vmem,
        compiler_params=pltpu.CompilerParams(vmem_limit_bytes=4 * 1024 * 1024),
        name="place_tiles",
    )(me.reshape(1), tiles)


def body(activations, cotangents, token_ids, signs, select):
    n_param, n_group = lax.axis_size("param"), lax.axis_size("ex")
    n_ex, _, width = activations.shape
    me = lax.axis_index("param")
    table = make_table(activations, cotangents, token_ids, signs)
    index = make_index(select, me, n_param, width, table)
    n_block = select.shape[0] // n_param // LANES
    n_y = n_param // 2
    swap = [(i, i ^ 1) for i in range(n_param)]

    def along(step):
        return [(i, (i + 2 * step) % n_param) for i in range(n_param)]

    mid = n_block // 2
    sent = gather_rows(table, index, 0, FAR)
    arrived = lax.ppermute(sent, "param", swap)
    outward = gather_rows(table, index, 1, FAR, after=(sent,)) + arrived
    opposite = lax.ppermute(outward, "param", along(2))
    near, outward = [], (outward,)
    for group in (FIRST, SECOND):
        sent = gather_rows(table, index, 0, group, after=outward)
        arrived = lax.ppermute(sent, "param", swap)
        kept = gather_rows(table, index, 1, group, after=(sent,))
        outward = (kept[:mid] + arrived[:mid], kept[mid:] + arrived[mid:])
        near.append(
            lax.ppermute(outward[0], "param", along(1)) + lax.ppermute(outward[1], "param", along(-1))
        )
    sent = gather_rows(table, index, 0, OWN, after=outward)
    arrived = lax.ppermute(sent, "param", swap)
    own = gather_rows(table, index, 1, OWN, after=(sent,))
    front = own[:mid] + arrived[:mid] + opposite[:mid] + near[0]
    own, arrived, opposite, front = lax.optimization_barrier((own, arrived, opposite, front))
    back = own[mid:] + arrived[mid:] + opposite[mid:] + near[1]
    features = (front, back)
    shares = [lax.all_to_all(x, "ex", split_axis=0, concat_axis=0) for x in features]
    shares += [lax.ppermute(x, "param", swap) for x in shares]
    whole_features = jnp.swapaxes(jnp.concatenate(features, axis=0), 0, 1).reshape(n_ex, -1)

    partial = partial_gram(shares, me % 2)
    rows_out = partial.shape[2]
    everyone = ("param", "ex")
    alike = [
        [(2 * y + core) * n_group + e for y in range(n_y) for e in range(n_group)] for core in range(2)
    ]
    received = lax.all_to_all(
        partial.reshape(n_y * n_group, rows_out, LANES),
        everyone,
        split_axis=0,
        concat_axis=0,
        axis_index_groups=alike,
    )
    tile, turned = sum_tiles(received)
    onward = [
        (p * n_group + e, p * n_group + (e + p + 1) % n_group) for p in range(n_param) for e in range(n_group)
    ]
    turned = lax.ppermute(turned, everyone, onward)
    spread = lax.all_to_all(
        messages(tile, turned, diagonal_part(features), n_param), "param", split_axis=0, concat_axis=0
    )
    gram = place_tiles(spread, lax.axis_index("ex"), n_ex, n_group)
    return (whole_features, gram)


def solution(mesh):
    return jax.shard_map(
        body,
        mesh=mesh,
        in_specs=(
            P("ex", None, "param"),
            P("ex", None, None),
            P("ex", None),
            P(None, "param"),
            P(),
        ),
        out_specs=(P("ex", "param"), P("ex", None)),
        check_vma=False,
    )
```

```python
import functools
import math

import jax
import jax.numpy as jnp
import ml_dtypes
import numpy as np
from jax import lax
from jax.experimental import pallas as pl
from jax.experimental.pallas import tpu as pltpu
from jax.sharding import PartitionSpec as P

D = 8192
SLAB = 64
TOKS = 128
K = 32768
LANES = 128
ROW_COST = 10_000_000
STEP_EX = 8
TAP = 256
EXTRA_ROWS = 8


def walsh_table(order):
    table = np.ones((1, 1), np.float32)
    while table.shape[0] < order:
        table = np.block([[table, table], [table, -table]])
    return table.astype(ml_dtypes.bfloat16)


def butterfly(parts):
    count = len(parts)
    half = 1
    while half < count:
        out = list(parts)
        for index in range(count):
            if not index & half:
                out[index] = parts[index] + parts[index | half]
                out[index | half] = parts[index] - parts[index | half]
        parts = out
        half *= 2
    return parts


def table_kernel(n_ex, width, acts_ref, *refs):
    sources, (table_ref, grad_ref, flip_ref), copies, sems = refs[:4], refs[4:7], refs[7:11], refs[11]
    cots_ref, ids_ref, signs_ref, walsh_ref = copies
    step = pl.program_id(0)
    tiles = width // LANES
    rows = SLAB
    stride = SLAB + EXTRA_ROWS

    @pl.when(step == 0)
    def _():
        started = [pltpu.make_async_copy(a, b, sems.at[i]) for i, (a, b) in enumerate(zip(sources, copies))]
        for copy in started:
            copy.start()
        for copy in started:
            copy.wait()
        factor = 1.0 / math.sqrt(TOKS) / math.sqrt(SLAB * D)
        flip_ref[...] = signs_ref[...].astype(jnp.float32) * factor

    @pl.loop(0, STEP_EX, unroll=4)
    def _(i):
        e = step * STEP_EX + i
        live = (ids_ref[pl.ds(e, 1), :] != 0).astype(jnp.bfloat16)
        g = jnp.dot(cots_ref[e] * live, acts_ref[i], preferred_element_type=jnp.float32)
        g = g * flip_ref[...]
        for low in range(2):
            tile = [g[:, (2 * q + low) * LANES:(2 * q + low + 1) * LANES] for q in range(tiles // 2)]
            tile = butterfly(tile)
            for q in range(tiles // 2):
                parts = butterfly([tile[q][8 * s:8 * s + 8] for s in range(rows // 8)])
                for s in range(rows // 8):
                    grad_ref[2 * q + low, pl.ds(e * stride + 8 * s, 8), :] = parts[s]

    @pl.when(step == pl.num_programs(0) - 1)
    def _():
        lane = lax.broadcasted_iota(jnp.int32, (TAP, LANES), 1)
        low_half = jnp.where(lane < LANES // 2, 1.0, -1.0).astype(jnp.float32)

        @pl.loop(0, (rows // 8) * (tiles // 2), unroll=4)
        def _(index):
            s = index // (tiles // 2)
            q = index % (tiles // 2)
            high, low = [], []
            for r in range(8):
                pieces = [
                    grad_ref.at[2 * q + j][pl.ds(s * 8 + r, n_ex, stride=stride), :] for j in range(2)
                ]
                x = jnp.concatenate(pieces, axis=1)
                h = x.astype(jnp.bfloat16)
                high.append(h)
                low.append((x - h.astype(jnp.float32)).astype(jnp.bfloat16))
            nt = (((1,), (1,)), ((), ()))
            mixed = lax.dot_general(walsh_ref[...], jnp.concatenate(high, axis=0), nt, preferred_element_type=jnp.float32)
            mixed += lax.dot_general(walsh_ref[...], jnp.concatenate(low, axis=0), nt, preferred_element_type=jnp.float32)
            parts = butterfly([mixed[:, j * LANES:(j + 1) * LANES] for j in range(4)])
            for j in range(4):
                v = parts[j]
                v = v * low_half + pltpu.roll(v, LANES // 2, 1)
                table_ref[pl.ds((s * 4 + j) * width + q * TAP, TAP), :] = v


def gather_kernel(start, rows_ref, table_ref, half_ref, sign_ref, *refs):
    out_ref, bufs = refs[-3], refs[-2:]
    n_block = out_ref.shape[0]

    def fetch(block, slot):
        base = pl.multiple_of(block * LANES, LANES)
        for j in range(LANES):
            bufs[slot][j:j + 1, :] = table_ref[pl.ds(rows_ref[base + j], 1), :]

    def finish(block, t):
        here = pl.ds(start + block, 1)
        picked = jnp.where(half_ref[here, :] > 0, t[LANES // 2:], t[:LANES // 2])
        out_ref[block] = picked * sign_ref[here, :]

    fetch(0, 0)

    @pl.loop(0, n_block // 2)
    def _(i):
        t = bufs[0][...].T
        fetch(2 * i + 1, 1)
        finish(2 * i, t)
        t = bufs[1][...].T
        fetch(jnp.minimum(2 * i + 2, n_block - 1), 0)
        finish(2 * i + 1, t)


def whole(shape):
    return pl.BlockSpec(shape, lambda i, *_: (0,) * len(shape))


def make_table(activations, cotangents, token_ids, signs):
    n_ex, toks, width = activations.shape
    slab = cotangents.shape[2]
    small = [
        pltpu.with_memory_space_constraint(x, pltpu.HBM)
        for x in (jnp.swapaxes(cotangents, 1, 2), token_ids, signs, jnp.asarray(walsh_table(TAP)))
    ]
    return pl.pallas_call(
        functools.partial(table_kernel, n_ex, width),
        out_shape=pltpu.VMEM((slab // 2 * width, LANES), jnp.float32),
        grid=(n_ex // STEP_EX,),
        in_specs=[
            pl.BlockSpec((STEP_EX, toks, width), lambda i: (i, 0, 0)),
        ] + [pl.BlockSpec(memory_space=pltpu.HBM)] * 4,
        out_specs=pl.BlockSpec(memory_space=pltpu.VMEM),
        scratch_shapes=[
            pltpu.VMEM((width // LANES, n_ex * (slab + EXTRA_ROWS), LANES), jnp.float32),
            pltpu.VMEM((slab, width), jnp.float32),
            pltpu.VMEM((n_ex, slab, toks), cotangents.dtype),
            pltpu.VMEM(token_ids.shape, token_ids.dtype),
            pltpu.VMEM(signs.shape, signs.dtype),
            pltpu.VMEM((TAP, TAP), jnp.bfloat16),
            pltpu.SemaphoreType.DMA((4,)),
        ],
        compiler_params=pltpu.CompilerParams(
            dimension_semantics=("arbitrary",), vmem_limit_bytes=26 * 1024 * 1024
        ),
        cost_estimate=pl.CostEstimate(flops=10**13, bytes_accessed=2**25, transcendentals=0),
        name="make_table",
    )(activations, *small)


def gather_rows(table, index, core, group, after=()):
    half, sign = index[:2]
    rows = index[2 + core * len(GROUPS) + group]
    n_block = rows.shape[0]
    start = (core * len(GROUPS) + group) * n_block
    vmem = pl.BlockSpec(memory_space=pltpu.VMEM)
    return pl.pallas_call(
        functools.partial(gather_kernel, start),
        out_shape=jax.ShapeDtypeStruct((n_block, LANES // 2, LANES), jnp.float32),
        in_specs=[pl.BlockSpec(memory_space=pltpu.SMEM)] + [vmem] * 3
        + [pl.BlockSpec(memory_space=pl.ANY)] * len(after),
        out_specs=vmem,
        scratch_shapes=[pltpu.VMEM((LANES, LANES), jnp.float32)] * 2,
        compiler_params=pltpu.CompilerParams(vmem_limit_bytes=4 * 1024 * 1024),
        cost_estimate=pl.CostEstimate(
            flops=n_block * LANES * ROW_COST, bytes_accessed=n_block * LANES * 4096, transcendentals=0
        ),
        name="gather_rows",
    )(rows.reshape(-1), table, half, sign, *after)


GROUPS = (((2, 0), (2, 1)), ((1, 0), (3, 0)), ((1, 1), (3, 1)), ((0, 0), (0, 1)))
FAR, FIRST, SECOND, OWN = range(4)


def index_kernel(width, bits, me_ref, select_ref, table_ref, half_ref, sign_ref, *rows_refs):
    me = me_ref[0]
    n_y, _, n_block, _ = select_ref.shape
    mid = n_block // 2
    col_bits, width_bits = D.bit_length() - 1, width.bit_length() - 1
    for core in range(2):
        owner_core = (me & 1) ^ (1 - core)
        for group, pieces in enumerate(GROUPS):
            for place, (step, part) in enumerate(pieces):
                chosen = select_ref[((me >> 1) + step) & (n_y - 1), owner_core, part * mid:(part + 1) * mid, :]
                row = chosen >> col_bits
                column = chosen & (D - 1)
                shared = (column >> width_bits) & me
                parity = jnp.zeros_like(shared)
                for bit in range(bits):
                    parity = parity ^ (shared >> bit & 1)
                here = pl.ds((core * len(GROUPS) + group) * n_block + place * mid, mid)
                rows = (row >> 1) * width + (column & (width - 1))
                rows_refs[core * len(GROUPS) + group][place * mid:(place + 1) * mid, :] = rows
                half_ref[here, :] = row & 1
                sign_ref[here, :] = (1 - 2 * parity).astype(jnp.float32)


def make_index(select, me, n_param, width, after):
    n_block = select.shape[0] // LANES
    vmem = pl.BlockSpec(memory_space=pltpu.VMEM)
    return pl.pallas_call(
        functools.partial(index_kernel, width, n_param.bit_length() - 1),
        out_shape=(
            jax.ShapeDtypeStruct((n_block, LANES), jnp.int32),
            jax.ShapeDtypeStruct((n_block, LANES), jnp.float32),
        ) + (jax.ShapeDtypeStruct((n_block // n_param, LANES), jnp.int32),) * n_param,
        in_specs=[pl.BlockSpec(memory_space=pltpu.SMEM), vmem, pl.BlockSpec(memory_space=pl.ANY)],
        out_specs=(vmem,) * (2 + n_param),
        compiler_params=pltpu.CompilerParams(vmem_limit_bytes=4 * 1024 * 1024),
        name="make_index",
    )(me.reshape(1), select.reshape(n_param // 2, 2, n_block // n_param, LANES), after)


def gram_kernel(n_ex, core_ref, *refs):
    x_refs, out_ref, high_ref, low_ref, part_ref = refs[:-4], refs[-4], refs[-3], refs[-2], refs[-1]
    core = core_ref[0]
    blocks = x_refs[0].shape[0]
    half = LANES // 2
    for b in range(blocks):
        x = jnp.concatenate([r[b] for r in x_refs], axis=1)
        h = x.astype(jnp.bfloat16)
        low = (x - h.astype(jnp.float32)).astype(jnp.bfloat16)
        for at in ((b + 8, b - 8) if b >= 8 else (b + 8,)):
            high_ref[at * n_ex:(at + 1) * n_ex, :] = h
            low_ref[at * n_ex:(at + 1) * n_ex, :] = low
    left = lax.broadcasted_iota(jnp.int32, (n_ex // 2, LANES), 1) < half
    nt = (((1,), (1,)), ((), ()))

    @pl.loop(0, blocks // 4)
    def _(quad):
        rows = pl.ds(pl.multiple_of(quad * 4 * n_ex, 4 * n_ex), 12 * n_ex)
        columns = pl.ds(pl.multiple_of((quad * 4 + 8) * n_ex, 4 * n_ex), 4 * n_ex)
        t = lax.dot_general(high_ref[rows, :], high_ref[columns, :], nt, preferred_element_type=jnp.float32)
        t += lax.dot_general(high_ref[rows, :], low_ref[columns, :], nt, preferred_element_type=jnp.float32)
        t += lax.dot_general(low_ref[rows, :], high_ref[columns, :], nt, preferred_element_type=jnp.float32)
        part_ref[...] = t
        for v in range(4):
            lanes = slice(v // 2 * LANES, (v // 2 + 1) * LANES)
            for m in range(4):
                offset = 2 * m + core + 1
                first = pl.multiple_of((8 + v - offset) * n_ex, n_ex)
                top = part_ref[pl.ds(first, n_ex // 2), lanes]
                low = part_ref[pl.ds(first + n_ex // 2, n_ex // 2), lanes]
                if v % 2:
                    top = pltpu.roll(top, half, 1)
                else:
                    low = pltpu.roll(low, half, 1)
                row_block = (quad * 4 + v + blocks - offset) & (blocks - 1)
                out_ref[m, row_block] = jnp.where(left, top, low)


def partial_gram(shares, core):
    blocks, n_ex, _ = shares[0].shape
    width = len(shares) * LANES
    vmem = pl.BlockSpec(memory_space=pltpu.VMEM)
    return pl.pallas_call(
        functools.partial(gram_kernel, n_ex),
        out_shape=jax.ShapeDtypeStruct((4, blocks, n_ex // 2, LANES), jnp.float32),
        in_specs=[pl.BlockSpec(memory_space=pltpu.SMEM)] + [vmem] * len(shares),
        out_specs=vmem,
        scratch_shapes=[pltpu.VMEM(((blocks + 8) * n_ex, width), jnp.bfloat16)] * 2
        + [pltpu.VMEM((12 * n_ex, 4 * n_ex), jnp.float32)],
        compiler_params=pltpu.CompilerParams(vmem_limit_bytes=16 * 1024 * 1024),
        name="partial_gram",
    )(core.reshape(1), *shares)


def halves_side_by_side(tile):
    rows = tile.shape[0] // 2
    return jnp.concatenate([tile[:rows], tile[rows:]], axis=1)


def halves_stacked(pair):
    lanes = pair.shape[1] // 2
    return jnp.concatenate([pair[:, :lanes], pair[:, lanes:]], axis=0)


def diagonal_kernel(*refs):
    out_ref = refs[-1]
    nt = (((1,), (1,)), ((), ()))
    same = cross = 0.0
    for ref in refs[:-1]:
        x = jnp.concatenate([ref[b] for b in range(ref.shape[0])], axis=1)
        high = x.astype(jnp.bfloat16)
        low = (x - high.astype(jnp.float32)).astype(jnp.bfloat16)
        same += lax.dot_general(high, high, nt, preferred_element_type=jnp.float32)
        cross += lax.dot_general(high, low, nt, preferred_element_type=jnp.float32)
    out_ref[...] = halves_side_by_side((same + cross + cross.T) * (1.0 / K))


def diagonal_part(features):
    n_ex = features[0].shape[1]
    vmem = pl.BlockSpec(memory_space=pltpu.VMEM)
    return pl.pallas_call(
        diagonal_kernel,
        out_shape=jax.ShapeDtypeStruct((n_ex // 2, 2 * n_ex), jnp.float32),
        in_specs=[vmem] * len(features),
        out_specs=vmem,
        compiler_params=pltpu.CompilerParams(vmem_limit_bytes=8 * 1024 * 1024),
        cost_estimate=pl.CostEstimate(flops=4 * 10**9, bytes_accessed=2**20, transcendentals=0),
        name="diagonal_part",
    )(*features)


def sum_kernel(x_ref, tile_ref, turned_ref):
    tile = halves_stacked(jnp.sum(x_ref[...], axis=0) * (1.0 / K))
    tile_ref[...] = tile
    turned_ref[...] = tile.T


def sum_tiles(received):
    n_ex = 2 * received.shape[1]
    vmem = pl.BlockSpec(memory_space=pltpu.VMEM)
    return pl.pallas_call(
        sum_kernel,
        out_shape=(jax.ShapeDtypeStruct((n_ex, n_ex), jnp.float32),) * 2,
        in_specs=[vmem],
        out_specs=(vmem, vmem),
        compiler_params=pltpu.CompilerParams(vmem_limit_bytes=4 * 1024 * 1024),
        name="sum_tiles",
    )(received)


def message_kernel(tile_ref, turned_ref, part_ref, out_ref):
    n_ex = tile_ref.shape[0]
    pair = jnp.concatenate([tile_ref[...], turned_ref[...]], axis=1)
    for p in range(out_ref.shape[0]):
        out_ref[p, :n_ex, :] = pair
        out_ref[p, n_ex:, :] = part_ref[...]


def messages(tile, turned, part, count):
    rows = tile.shape[0] + part.shape[0]
    vmem = pl.BlockSpec(memory_space=pltpu.VMEM)
    return pl.pallas_call(
        message_kernel,
        out_shape=jax.ShapeDtypeStruct((count, rows, LANES), jnp.float32),
        in_specs=[vmem] * 3,
        out_specs=vmem,
        compiler_params=pltpu.CompilerParams(vmem_limit_bytes=4 * 1024 * 1024),
        name="messages",
    )(tile, turned, part)


def place_kernel(me_ref, x_ref, out_ref):
    half = LANES // 2
    count = out_ref.shape[1] // half
    columns = [None] * count
    columns[0] = halves_stacked(jnp.sum(x_ref[:, half:, :], axis=0))
    for p in range(8):
        columns[p + 1] = x_ref[p, :half, :half]
        if count - 1 - p > p + 1:
            columns[count - 1 - p] = x_ref[p, :half, half:]
    row = jnp.concatenate(columns, axis=1)
    out_ref[...] = pltpu.roll(row, me_ref[0] * half, 1)


def place_tiles(tiles, me, n_ex, count):
    vmem = pl.BlockSpec(memory_space=pltpu.VMEM)
    return pl.pallas_call(
        place_kernel,
        out_shape=jax.ShapeDtypeStruct((n_ex, count * n_ex), jnp.float32),
        in_specs=[pl.BlockSpec(memory_space=pltpu.SMEM), vmem],
        out_specs=vmem,
        compiler_params=pltpu.CompilerParams(vmem_limit_bytes=4 * 1024 * 1024),
        name="place_tiles",
    )(me.reshape(1), tiles)


def join_kernel(first, n_terms, *refs):
    out_ref = refs[-1]
    n_block = out_ref.shape[0]

    @pl.loop(0, n_block)
    def _(b):
        total = 0.0
        for ref in refs[:n_terms]:
            total += ref[b + (first if ref.shape[0] > n_block else 0)]
        out_ref[b] = total


def join(first, count, terms, after=()):
    vmem = pl.BlockSpec(memory_space=pltpu.VMEM)
    return pl.pallas_call(
        functools.partial(join_kernel, first, len(terms)),
        out_shape=jax.ShapeDtypeStruct((count,) + terms[0].shape[1:], jnp.float32),
        in_specs=[vmem] * len(terms) + [pl.BlockSpec(memory_space=pl.ANY)] * len(after),
        out_specs=vmem,
        compiler_params=pltpu.CompilerParams(vmem_limit_bytes=4 * 1024 * 1024),
        name="join",
    )(*terms, *after)


def body(activations, cotangents, token_ids, signs, select):
    n_param, n_group = lax.axis_size("param"), lax.axis_size("ex")
    n_ex, _, width = activations.shape
    me = lax.axis_index("param")
    table = make_table(activations, cotangents, token_ids, signs)
    index = make_index(select, me, n_param, width, table)
    n_block = select.shape[0] // n_param // LANES
    n_y = n_param // 2
    swap = [(i, i ^ 1) for i in range(n_param)]

    def along(step):
        return [(i, (i + 2 * step) % n_param) for i in range(n_param)]

    mid = n_block // 2
    sent = gather_rows(table, index, 0, FAR)
    arrived = lax.ppermute(sent, "param", swap)
    outward = gather_rows(table, index, 1, FAR, after=(sent,)) + arrived
    opposite = lax.ppermute(outward, "param", along(2))
    near, outward = [], (outward,)
    for group in (FIRST, SECOND):
        sent = gather_rows(table, index, 0, group, after=outward)
        arrived = lax.ppermute(sent, "param", swap)
        kept = gather_rows(table, index, 1, group, after=(sent,))
        outward = (kept[:mid] + arrived[:mid], kept[mid:] + arrived[mid:])
        near.append(
            (lax.ppermute(outward[0], "param", along(1)), lax.ppermute(outward[1], "param", along(-1)))
        )
    sent = gather_rows(table, index, 0, OWN, after=outward)
    arrived = lax.ppermute(sent, "param", swap)
    own = gather_rows(table, index, 1, OWN, after=(sent,))
    front = join(0, mid, (own, arrived, opposite, *near[0]))
    back = join(mid, mid, (own, arrived, opposite, *near[1]), after=(front,))
    features = (front, back)
    shares = [lax.all_to_all(x, "ex", split_axis=0, concat_axis=0) for x in features]
    shares += [lax.ppermute(x, "param", swap) for x in shares]
    whole_features = jnp.swapaxes(jnp.concatenate(features, axis=0), 0, 1).reshape(n_ex, -1)

    partial = partial_gram(shares, me % 2)
    rows_out = partial.shape[2]
    everyone = ("param", "ex")
    alike = [
        [(2 * y + core) * n_group + e for y in range(n_y) for e in range(n_group)] for core in range(2)
    ]
    received = lax.all_to_all(
        partial.reshape(n_y * n_group, rows_out, LANES),
        everyone,
        split_axis=0,
        concat_axis=0,
        axis_index_groups=alike,
    )
    tile, turned = sum_tiles(received)
    onward = [
        (p * n_group + e, p * n_group + (e + p + 1) % n_group) for p in range(n_param) for e in range(n_group)
    ]
    turned = lax.ppermute(turned, everyone, onward)
    spread = lax.all_to_all(
        messages(tile, turned, diagonal_part(features), n_param), "param", split_axis=0, concat_axis=0
    )
    gram = place_tiles(spread, lax.axis_index("ex"), n_ex, n_group)
    return (whole_features, gram)


def solution(mesh):
    return jax.shard_map(
        body,
        mesh=mesh,
        in_specs=(
            P("ex", None, "param"),
            P("ex", None, None),
            P("ex", None),
            P(None, "param"),
            P(),
        ),
        out_specs=(P("ex", "param"), P("ex", None)),
        check_vma=False,
    )
```

```python
import functools
import math

import jax
import jax.numpy as jnp
import ml_dtypes
import numpy as np
from jax import lax
from jax.experimental import pallas as pl
from jax.experimental.pallas import tpu as pltpu
from jax.sharding import PartitionSpec as P

D = 8192
SLAB = 64
TOKS = 128
K = 32768
LANES = 128
ROW_COST = 10_000_000
STEP_EX = 8
TAP = 256
EXTRA_ROWS = 8


def walsh_table(order):
    table = np.ones((1, 1), np.float32)
    while table.shape[0] < order:
        table = np.block([[table, table], [table, -table]])
    return table.astype(ml_dtypes.bfloat16)


def butterfly(parts):
    count = len(parts)
    half = 1
    while half < count:
        out = list(parts)
        for index in range(count):
            if not index & half:
                out[index] = parts[index] + parts[index | half]
                out[index | half] = parts[index] - parts[index | half]
        parts = out
        half *= 2
    return parts


def table_kernel(n_ex, width, acts_ref, *refs):
    sources, (table_ref, grad_ref, flip_ref), copies, sems = refs[:4], refs[4:7], refs[7:11], refs[11]
    cots_ref, ids_ref, signs_ref, walsh_ref = copies
    step = pl.program_id(0)
    tiles = width // LANES
    rows = SLAB
    stride = SLAB + EXTRA_ROWS

    @pl.when(step == 0)
    def _():
        started = [pltpu.make_async_copy(a, b, sems.at[i]) for i, (a, b) in enumerate(zip(sources, copies))]
        for copy in started:
            copy.start()
        for copy in started:
            copy.wait()
        factor = 1.0 / math.sqrt(TOKS) / math.sqrt(SLAB * D)
        flip_ref[...] = signs_ref[...].astype(jnp.float32) * factor

    @pl.loop(0, STEP_EX, unroll=4)
    def _(i):
        e = step * STEP_EX + i
        live = (ids_ref[pl.ds(e, 1), :] != 0).astype(jnp.bfloat16)
        g = jnp.dot(cots_ref[e] * live, acts_ref[i], preferred_element_type=jnp.float32)
        g = g * flip_ref[...]
        for low in range(2):
            tile = [g[:, (2 * q + low) * LANES:(2 * q + low + 1) * LANES] for q in range(tiles // 2)]
            tile = butterfly(tile)
            for q in range(tiles // 2):
                parts = butterfly([tile[q][8 * s:8 * s + 8] for s in range(rows // 8)])
                for s in range(rows // 8):
                    grad_ref[2 * q + low, pl.ds(e * stride + 8 * s, 8), :] = parts[s]

    @pl.when(step == pl.num_programs(0) - 1)
    def _():
        lane = lax.broadcasted_iota(jnp.int32, (TAP, LANES), 1)
        low_half = jnp.where(lane < LANES // 2, 1.0, -1.0).astype(jnp.float32)

        @pl.loop(0, (rows // 8) * (tiles // 2), unroll=4)
        def _(index):
            s = index // (tiles // 2)
            q = index % (tiles // 2)
            high, low = [], []
            for r in range(8):
                pieces = [
                    grad_ref.at[2 * q + j][pl.ds(s * 8 + r, n_ex, stride=stride), :] for j in range(2)
                ]
                x = jnp.concatenate(pieces, axis=1)
                h = x.astype(jnp.bfloat16)
                high.append(h)
                low.append((x - h.astype(jnp.float32)).astype(jnp.bfloat16))
            nt = (((1,), (1,)), ((), ()))
            mixed = lax.dot_general(walsh_ref[...], jnp.concatenate(high, axis=0), nt, preferred_element_type=jnp.float32)
            mixed += lax.dot_general(walsh_ref[...], jnp.concatenate(low, axis=0), nt, preferred_element_type=jnp.float32)
            parts = butterfly([mixed[:, j * LANES:(j + 1) * LANES] for j in range(4)])
            for j in range(4):
                v = parts[j]
                v = v * low_half + pltpu.roll(v, LANES // 2, 1)
                table_ref[pl.ds((s * 4 + j) * width + q * TAP, TAP), :] = v


def gather_kernel(segments, start, rows_ref, table_ref, half_ref, sign_ref, *refs):
    n_extra = sum(extra is not None for _, _, extra in segments)
    extras, out_ref, bufs = refs[:n_extra], refs[-3], refs[-2:]
    n_block = segments[-1][1]

    def fetch(block, slot):
        base = pl.multiple_of(block * LANES, LANES)
        for j in range(LANES):
            bufs[slot][j:j + 1, :] = table_ref[pl.ds(rows_ref[base + j], 1), :]

    def finish(block, t, extra, first):
        here = pl.ds(start + block, 1)
        picked = jnp.where(half_ref[here, :] > 0, t[LANES // 2:], t[:LANES // 2]) * sign_ref[here, :]
        out_ref[block] = picked if extra is None else picked + extras[extra][block - first]

    fetch(0, 0)
    for first, last, extra in segments:

        @pl.loop(first // 2, last // 2)
        def _(i):
            t = bufs[0][...].T
            fetch(2 * i + 1, 1)
            finish(2 * i, t, extra, first)
            t = bufs[1][...].T
            fetch(jnp.minimum(2 * i + 2, n_block - 1), 0)
            finish(2 * i + 1, t, extra, first)


def whole(shape):
    return pl.BlockSpec(shape, lambda i, *_: (0,) * len(shape))


def make_table(activations, cotangents, token_ids, signs):
    n_ex, toks, width = activations.shape
    slab = cotangents.shape[2]
    small = [
        pltpu.with_memory_space_constraint(x, pltpu.HBM)
        for x in (jnp.swapaxes(cotangents, 1, 2), token_ids, signs, jnp.asarray(walsh_table(TAP)))
    ]
    return pl.pallas_call(
        functools.partial(table_kernel, n_ex, width),
        out_shape=pltpu.VMEM((slab // 2 * width, LANES), jnp.float32),
        grid=(n_ex // STEP_EX,),
        in_specs=[
            pl.BlockSpec((STEP_EX, toks, width), lambda i: (i, 0, 0)),
        ] + [pl.BlockSpec(memory_space=pltpu.HBM)] * 4,
        out_specs=pl.BlockSpec(memory_space=pltpu.VMEM),
        scratch_shapes=[
            pltpu.VMEM((width // LANES, n_ex * (slab + EXTRA_ROWS), LANES), jnp.float32),
            pltpu.VMEM((slab, width), jnp.float32),
            pltpu.VMEM((n_ex, slab, toks), cotangents.dtype),
            pltpu.VMEM(token_ids.shape, token_ids.dtype),
            pltpu.VMEM(signs.shape, signs.dtype),
            pltpu.VMEM((TAP, TAP), jnp.bfloat16),
            pltpu.SemaphoreType.DMA((4,)),
        ],
        compiler_params=pltpu.CompilerParams(
            dimension_semantics=("arbitrary",), vmem_limit_bytes=26 * 1024 * 1024
        ),
        cost_estimate=pl.CostEstimate(flops=10**13, bytes_accessed=2**25, transcendentals=0),
        name="make_table",
    )(activations, *small)


def gather_rows(table, index, core, group, after=(), add=()):
    half, sign = index[:2]
    rows = index[2 + core * len(GROUPS) + group]
    n_block = rows.shape[0]
    start = (core * len(GROUPS) + group) * n_block
    segments, at = [], 0
    for number, (low, high, _) in enumerate(add):
        if at < low:
            segments.append((at, low, None))
        segments.append((low, high, number))
        at = high
    if at < n_block:
        segments.append((at, n_block, None))
    vmem = pl.BlockSpec(memory_space=pltpu.VMEM)
    n_add = len(add)

    def kernel(*refs):
        gather_kernel(segments, start, *refs[:4 + n_add], *refs[4 + n_add + len(after):])

    return pl.pallas_call(
        kernel,
        out_shape=jax.ShapeDtypeStruct((n_block, LANES // 2, LANES), jnp.float32),
        in_specs=[pl.BlockSpec(memory_space=pltpu.SMEM)] + [vmem] * (3 + n_add) + [pl.BlockSpec(memory_space=pl.ANY)] * len(after),
        out_specs=vmem,
        scratch_shapes=[pltpu.VMEM((LANES, LANES), jnp.float32)] * 2,
        compiler_params=pltpu.CompilerParams(vmem_limit_bytes=4 * 1024 * 1024),
        cost_estimate=pl.CostEstimate(
            flops=n_block * LANES * ROW_COST, bytes_accessed=n_block * LANES * 4096, transcendentals=0
        ),
        name="gather_rows",
    )(rows.reshape(-1), table, half, sign, *[x for _, _, x in add], *after)


GROUPS = (((2, 0), (2, 1)), ((1, 0), (3, 0)), ((1, 1), (3, 1)), ((0, 0), (0, 1)))
FAR, FIRST, SECOND, OWN = range(4)


def index_kernel(width, bits, me_ref, select_ref, table_ref, half_ref, sign_ref, *rows_refs):
    me = me_ref[0]
    n_y, _, n_block, _ = select_ref.shape
    mid = n_block // 2
    col_bits, width_bits = D.bit_length() - 1, width.bit_length() - 1
    for core in range(2):
        owner_core = (me & 1) ^ (1 - core)
        for group, pieces in enumerate(GROUPS):
            for place, (step, part) in enumerate(pieces):
                chosen = select_ref[((me >> 1) + step) & (n_y - 1), owner_core, part * mid:(part + 1) * mid, :]
                row = chosen >> col_bits
                column = chosen & (D - 1)
                shared = (column >> width_bits) & me
                parity = jnp.zeros_like(shared)
                for bit in range(bits):
                    parity = parity ^ (shared >> bit & 1)
                here = pl.ds((core * len(GROUPS) + group) * n_block + place * mid, mid)
                rows = (row >> 1) * width + (column & (width - 1))
                rows_refs[core * len(GROUPS) + group][place * mid:(place + 1) * mid, :] = rows
                half_ref[here, :] = row & 1
                sign_ref[here, :] = (1 - 2 * parity).astype(jnp.float32)


def make_index(select, me, n_param, width, after):
    n_block = select.shape[0] // LANES
    vmem = pl.BlockSpec(memory_space=pltpu.VMEM)
    return pl.pallas_call(
        functools.partial(index_kernel, width, n_param.bit_length() - 1),
        out_shape=(
            jax.ShapeDtypeStruct((n_block, LANES), jnp.int32),
            jax.ShapeDtypeStruct((n_block, LANES), jnp.float32),
        ) + (jax.ShapeDtypeStruct((n_block // n_param, LANES), jnp.int32),) * n_param,
        in_specs=[pl.BlockSpec(memory_space=pltpu.SMEM), vmem, pl.BlockSpec(memory_space=pl.ANY)],
        out_specs=(vmem,) * (2 + n_param),
        compiler_params=pltpu.CompilerParams(vmem_limit_bytes=4 * 1024 * 1024),
        name="make_index",
    )(me.reshape(1), select.reshape(n_param // 2, 2, n_block // n_param, LANES), after)


def gram_kernel(n_ex, core_ref, *refs):
    x_refs = refs[:-5]
    out_ref, high_ref, low_ref, part_ref = refs[-4:]
    core = core_ref[0]
    blocks = x_refs[0].shape[0]
    half = LANES // 2
    for b in range(blocks):
        x = jnp.concatenate([r[b] for r in x_refs], axis=1)
        h = x.astype(jnp.bfloat16)
        low = (x - h.astype(jnp.float32)).astype(jnp.bfloat16)
        for at in ((b + 8, b - 8) if b >= 8 else (b + 8,)):
            high_ref[at * n_ex:(at + 1) * n_ex, :] = h
            low_ref[at * n_ex:(at + 1) * n_ex, :] = low
    left = lax.broadcasted_iota(jnp.int32, (n_ex // 2, LANES), 1) < half
    nt = (((1,), (1,)), ((), ()))

    @pl.loop(0, blocks // 4)
    def _(quad):
        rows = pl.ds(pl.multiple_of(quad * 4 * n_ex, 4 * n_ex), 12 * n_ex)
        columns = pl.ds(pl.multiple_of((quad * 4 + 8) * n_ex, 4 * n_ex), 4 * n_ex)
        t = lax.dot_general(high_ref[rows, :], high_ref[columns, :], nt, preferred_element_type=jnp.float32)
        t += lax.dot_general(high_ref[rows, :], low_ref[columns, :], nt, preferred_element_type=jnp.float32)
        t += lax.dot_general(low_ref[rows, :], high_ref[columns, :], nt, preferred_element_type=jnp.float32)
        part_ref[...] = t
        for v in range(4):
            lanes = slice(v // 2 * LANES, (v // 2 + 1) * LANES)
            for m in range(4):
                offset = 2 * m + core + 1
                first = pl.multiple_of((8 + v - offset) * n_ex, n_ex)
                top = part_ref[pl.ds(first, n_ex // 2), lanes]
                low = part_ref[pl.ds(first + n_ex // 2, n_ex // 2), lanes]
                if v % 2:
                    top = pltpu.roll(top, half, 1)
                else:
                    low = pltpu.roll(low, half, 1)
                row_block = (quad * 4 + v + blocks - offset) & (blocks - 1)
                out_ref[m, row_block] = jnp.where(left, top, low)


def partial_gram(shares, core, after):
    blocks, n_ex, _ = shares[0].shape
    width = len(shares) * LANES
    vmem = pl.BlockSpec(memory_space=pltpu.VMEM)
    return pl.pallas_call(
        functools.partial(gram_kernel, n_ex),
        out_shape=jax.ShapeDtypeStruct((4, blocks, n_ex // 2, LANES), jnp.float32),
        in_specs=[pl.BlockSpec(memory_space=pltpu.SMEM)] + [vmem] * len(shares)
        + [pl.BlockSpec(memory_space=pl.ANY)],
        out_specs=vmem,
        scratch_shapes=[pltpu.VMEM(((blocks + 8) * n_ex, width), jnp.bfloat16)] * 2
        + [pltpu.VMEM((12 * n_ex, 4 * n_ex), jnp.float32)],
        compiler_params=pltpu.CompilerParams(vmem_limit_bytes=16 * 1024 * 1024),
        name="partial_gram",
    )(core.reshape(1), *shares, after)


def halves_side_by_side(tile):
    rows = tile.shape[0] // 2
    return jnp.concatenate([tile[:rows], tile[rows:]], axis=1)


def halves_stacked(pair):
    lanes = pair.shape[1] // 2
    return jnp.concatenate([pair[:, :lanes], pair[:, lanes:]], axis=0)


def diagonal_kernel(*refs):
    out_ref = refs[-1]
    nt = (((1,), (1,)), ((), ()))
    same = cross = 0.0
    for ref in refs[:-1]:
        x = jnp.concatenate([ref[b] for b in range(ref.shape[0])], axis=1)
        high = x.astype(jnp.bfloat16)
        low = (x - high.astype(jnp.float32)).astype(jnp.bfloat16)
        same += lax.dot_general(high, high, nt, preferred_element_type=jnp.float32)
        cross += lax.dot_general(high, low, nt, preferred_element_type=jnp.float32)
    out_ref[...] = halves_side_by_side((same + cross + cross.T) * (1.0 / K))


def diagonal_part(features):
    n_ex = features[0].shape[1]
    vmem = pl.BlockSpec(memory_space=pltpu.VMEM)
    return pl.pallas_call(
        diagonal_kernel,
        out_shape=jax.ShapeDtypeStruct((n_ex // 2, 2 * n_ex), jnp.float32),
        in_specs=[vmem] * len(features),
        out_specs=vmem,
        compiler_params=pltpu.CompilerParams(vmem_limit_bytes=8 * 1024 * 1024),
        cost_estimate=pl.CostEstimate(flops=4 * 10**9, bytes_accessed=2**20, transcendentals=0),
        name="diagonal_part",
    )(*features)


def sum_kernel(x_ref, tile_ref, turned_ref):
    tile = halves_stacked(jnp.sum(x_ref[...], axis=0) * (1.0 / K))
    tile_ref[...] = tile
    turned_ref[...] = tile.T


def sum_tiles(received):
    n_ex = 2 * received.shape[1]
    vmem = pl.BlockSpec(memory_space=pltpu.VMEM)
    return pl.pallas_call(
        sum_kernel,
        out_shape=(jax.ShapeDtypeStruct((n_ex, n_ex), jnp.float32),) * 2,
        in_specs=[vmem],
        out_specs=(vmem, vmem),
        compiler_params=pltpu.CompilerParams(vmem_limit_bytes=4 * 1024 * 1024),
        name="sum_tiles",
    )(received)


def message_kernel(tile_ref, turned_ref, part_ref, out_ref):
    n_ex = tile_ref.shape[0]
    pair = jnp.concatenate([tile_ref[...], turned_ref[...]], axis=1)
    for p in range(out_ref.shape[0]):
        out_ref[p, :n_ex, :] = pair
        out_ref[p, n_ex:, :] = part_ref[...]


def messages(tile, turned, part, count):
    rows = tile.shape[0] + part.shape[0]
    vmem = pl.BlockSpec(memory_space=pltpu.VMEM)
    return pl.pallas_call(
        message_kernel,
        out_shape=jax.ShapeDtypeStruct((count, rows, LANES), jnp.float32),
        in_specs=[vmem] * 3,
        out_specs=vmem,
        compiler_params=pltpu.CompilerParams(vmem_limit_bytes=4 * 1024 * 1024),
        name="messages",
    )(tile, turned, part)


def place_kernel(me_ref, x_ref, out_ref):
    half = LANES // 2
    count = out_ref.shape[1] // half
    columns = [None] * count
    columns[0] = halves_stacked(jnp.sum(x_ref[:, half:, :], axis=0))
    for p in range(8):
        columns[p + 1] = x_ref[p, :half, :half]
        if count - 1 - p > p + 1:
            columns[count - 1 - p] = x_ref[p, :half, half:]
    row = jnp.concatenate(columns, axis=1)
    out_ref[...] = pltpu.roll(row, me_ref[0] * half, 1)


def place_tiles(tiles, me, n_ex, count):
    vmem = pl.BlockSpec(memory_space=pltpu.VMEM)
    return pl.pallas_call(
        place_kernel,
        out_shape=jax.ShapeDtypeStruct((n_ex, count * n_ex), jnp.float32),
        in_specs=[pl.BlockSpec(memory_space=pltpu.SMEM), vmem],
        out_specs=vmem,
        compiler_params=pltpu.CompilerParams(vmem_limit_bytes=4 * 1024 * 1024),
        name="place_tiles",
    )(me.reshape(1), tiles)


def body(activations, cotangents, token_ids, signs, select):
    n_param, n_group = lax.axis_size("param"), lax.axis_size("ex")
    n_ex, _, width = activations.shape
    me = lax.axis_index("param")
    table = make_table(activations, cotangents, token_ids, signs)
    index = make_index(select, me, n_param, width, table)
    n_block = select.shape[0] // n_param // LANES
    n_y = n_param // 2
    swap = [(i, i ^ 1) for i in range(n_param)]

    def along(step):
        return [(i, (i + 2 * step) % n_param) for i in range(n_param)]

    mid = n_block // 2
    sent = gather_rows(table, index, 0, FAR)
    arrived = lax.ppermute(sent, "param", swap)
    far = gather_rows(table, index, 1, FAR, after=(sent,))
    outward = (far[:mid] + arrived[:mid], far[mid:] + arrived[mid:])
    up, down = lax.ppermute(outward[0], "param", along(1)), lax.ppermute(outward[1], "param", along(-1))
    sent_first = gather_rows(table, index, 0, FIRST, after=outward)
    arrived_first = lax.ppermute(sent_first, "param", swap)
    sent_second = gather_rows(table, index, 0, SECOND, after=(sent_first,))
    arrived_second = lax.ppermute(sent_second, "param", swap)
    sent = gather_rows(table, index, 0, OWN, after=(sent_second,))
    arrived = lax.ppermute(sent, "param", swap)
    first = gather_rows(table, index, 1, FIRST, after=(sent,), add=((0, mid, up),))
    outward = (first[:mid] + arrived_first[:mid], first[mid:] + arrived_first[mid:])
    first = lax.ppermute(outward[0], "param", along(1)), lax.ppermute(outward[1], "param", along(-1))
    second = gather_rows(table, index, 1, SECOND, after=outward, add=((mid, n_block, down),))
    outward = (second[:mid] + arrived_second[:mid], second[mid:] + arrived_second[mid:])
    second = lax.ppermute(outward[0], "param", along(1)), lax.ppermute(outward[1], "param", along(-1))
    own = gather_rows(table, index, 1, OWN, after=outward)
    front = own[:mid] + arrived[:mid] + first[0] + first[1]
    own, arrived, front = lax.optimization_barrier((own, arrived, front))
    back = own[mid:] + arrived[mid:] + second[0] + second[1]
    features = (front, back)
    shares = [lax.all_to_all(x, "ex", split_axis=0, concat_axis=0) for x in features]
    shares += [lax.ppermute(x, "param", swap) for x in shares]
    whole_features = jnp.swapaxes(jnp.concatenate(features, axis=0), 0, 1).reshape(n_ex, -1)

    own_part = diagonal_part(features)
    partial = partial_gram(shares, me % 2, own_part)
    rows_out = partial.shape[2]
    everyone = ("param", "ex")
    alike = [
        [(2 * y + core) * n_group + e for y in range(n_y) for e in range(n_group)] for core in range(2)
    ]
    received = lax.all_to_all(
        partial.reshape(n_y * n_group, rows_out, LANES),
        everyone,
        split_axis=0,
        concat_axis=0,
        axis_index_groups=alike,
    )
    tile, turned = sum_tiles(received)
    onward = [
        (p * n_group + e, p * n_group + (e + p + 1) % n_group) for p in range(n_param) for e in range(n_group)
    ]
    turned = lax.ppermute(turned, everyone, onward)
    spread = lax.all_to_all(
        messages(tile, turned, own_part, n_param), "param", split_axis=0, concat_axis=0
    )
    gram = place_tiles(spread, lax.axis_index("ex"), n_ex, n_group)
    return (whole_features, gram)


def solution(mesh):
    return jax.shard_map(
        body,
        mesh=mesh,
        in_specs=(
            P("ex", None, "param"),
            P("ex", None, None),
            P("ex", None),
            P(None, "param"),
            P(),
        ),
        out_specs=(P("ex", "param"), P("ex", None)),
        check_vma=False,
    )
```
